32 devices in a mesh: dp: 4 (over y, core), outer: 8 (over z, x).
Axes of the slice: x: 2, y: 2, z: 4, core: 2. Of those that a mesh axis runs over, the one named last changes fastest.
Arguments:
- table: bfloat16 [131072, 256], P(('dp', 'outer')), may hold values from -5 to 5
- source_id: int32 [32768], P(('dp', 'outer')), may hold values from 0 to 15, as said below
- task_mask: int32 [16, 4], replicated, may hold values from 0 to 1, as said below
- feature_owner: int32 [32768, 2], P(('dp', 'outer')), may hold values from 0 to 31, all different within a row; in each aligned block of 1024 rows (0 to 1023, 1024 to 2047, ...) at most 128 rows name the same one
- feature_row: int32 [32768, 2], P(('dp', 'outer')), may hold values from 0 to 4095
- w_in: bfloat16 [4, 256, 1024], replicated, may hold values from -0.375 to 0.375
- b_in: bfloat16 [4, 1024], replicated, may hold values from -0.59765625 to 0.59765625
- w_out: bfloat16 [4, 1024, 256], replicated, may hold values from -0.1875 to 0.1875
- b_out: bfloat16 [4, 256], replicated, may hold values from -0.59765625 to 0.59765625
- select_weight: bfloat16 [256, 32], replicated, may hold values from -1 to 1
- mix_weight: bfloat16 [256, 16], replicated, may hold values from -0.1796875 to 0.1796875
- cotangent: bfloat16 [32768, 4, 256], P(('dp', 'outer')), may hold values from -6 to 6
Outputs:
- mixed: bfloat16 [32768, 4, 256], P(('dp', 'outer'))
- table_grad: float32 [131072, 256], P(('dp', 'outer'))
- w_in_grad: float32 [4, 256, 1024], replicated
- b_in_grad: float32 [4, 1024], replicated
- w_out_grad: float32 [4, 1024, 256], replicated
- b_out_grad: float32 [4, 256], replicated
- select_grad: float32 [256, 32], replicated
- mix_grad: float32 [256, 16], replicated
- entropy_mean: float32 [], replicated
The draws below stay inside these ranges and needn't reach their ends.
Inputs may be any that keep to these rules, and one draw needn't show every extreme that they name: `source_id`: the sources of one device's rows lie within 4 consecutive ids. `task_mask`: source s has exactly 1 + (4 * s) // 16 ones. `feature_owner`: in the 1024 rows of one device no owner is named more than 128 times, a bound that some block reaches; the 2 owners of a row differ.
All inputs are finite; a program needn't handle non-finite values.
Results may differ from the reference program's by a relative error of at most 0.0074.
Values may be sent and summed in bfloat16 or wider, within the bound.
No kernel may reach another device: no remote copies, remote signals or barrier semaphores. Data moves between devices by JAX's collectives and lax.ppermute only.
A program may use at most 128 MiB of HBM per device.

```python
import math
import jax
import jax.numpy as jnp
import numpy as np
from jax import lax

D = 256
H = 1024
EXPERTS = 4
BITS = 2
KSEL = 4
NTASK = 4
NSRC = 16
NF = 2
VOCAB_DEV = 4096
ROWS_DEV = 1024
ROWS = 32768
VOCAB = 131072
CAP = 128
DEVICES = 32


def draw_source_id(key, part):
    key = jax.random.fold_in(key, 11)
    positions = jnp.arange(ROWS, dtype=jnp.int32)
    device_place = positions // ROWS_DEV
    lowest = device_place * (3 * NSRC // 4) // max(DEVICES - 1, 1)
    offsets = jax.random.randint(key, (ROWS,), 0, NSRC // 4)
    return (lowest + offsets).astype(jnp.int32)


def draw_task_mask(key, part):
    key = jax.random.fold_in(key, 23)
    scores = jax.random.randint(key, (NSRC, NTASK), 0, 1 << 20) * NTASK + jnp.arange(NTASK, dtype=jnp.int32)[None, :]
    ranks = jnp.argsort(jnp.argsort(scores, axis=1), axis=1)
    task_count = 1 + NTASK * jnp.arange(NSRC, dtype=jnp.int32) // NSRC
    return (ranks < task_count[:, None]).astype(jnp.int32)


def plant(array, rng, least, high):
    longest = array.shape.index(max(array.shape))
    spots = []
    for shift in (0, 1):
        where = [jax.random.randint(jax.random.fold_in(rng, axis), (), 0, length) for axis, length in enumerate(array.shape)]
        where[longest] = (where[longest] + shift) % array.shape[longest]
        spots.append(tuple(where))
    return array.at[spots[0]].set(least).at[spots[1]].set(high)


def block_scale(own_key, shape, cuts, least, top_value):
    loudness = 1.0
    for position, shards_of in cuts:
        draws = jax.random.uniform(jax.random.fold_in(jax.random.fold_in(own_key, 6), position), (shards_of,), jnp.float32, least / len(cuts), top_value / len(cuts))
        loudness = loudness * jnp.repeat(jnp.exp(draws), shape[position] // shards_of).reshape((-1,) + (1,) * (len(shape) - 1 - position))
    return loudness


def rank_bounds(count, lean):
    loads = [(1 << 20) // math.isqrt(standing ** lean) + 1 for standing in range(1, count + 1)]
    spread = 1 + sum(loads) // (1 << 30)
    return np.cumsum(np.array([max(1, weight // spread) for weight in loads]))


def ranked(key, shape, number_of, lean):
    listing = rank_bounds(number_of, lean)
    pick = jax.random.randint(jax.random.fold_in(key, 1), shape, 0, int(listing[number_of - 1]))
    rank = jnp.searchsorted(jnp.asarray(listing, jnp.int32), pick, side="right")
    return jax.random.permutation(jax.random.fold_in(key, 2), number_of)[rank].astype(jnp.int32)


def routed_block(key, own, number, rows, amount, top, bound, lean):
    order = jax.random.permutation(key, amount)
    heavy_load, common = portions_of(amount, rows * top, bound, lean, True), portions_of(amount, rows * top, bound, lean, False)
    places = jnp.arange(amount)

    def named(tallies, offset_by):
        used = int((tallies > 0).sum())
        fixed = max(1, used // 4)
        shifted = fixed + (places - fixed + offset_by * (used - fixed)) % max(1, amount - fixed)
        return jnp.zeros((amount,), jnp.int32).at[order[jnp.where(places < fixed, places, shifted)]].set(jnp.asarray(tallies, jnp.int32))

    tallies = jnp.where(number % 4 == 0, named(heavy_load, number // 4), named(common, number - number // 4 - 1))
    mixed = jax.random.permutation(jax.random.fold_in(own, 3), amount)
    donor, sink = mixed[0:amount // 2 * 2:2], mixed[1:amount // 2 * 2:2]
    slack = jnp.minimum(tallies[donor] - 1, bound - tallies[sink]) // 2
    slack = jnp.where((donor == order[0]) | (sink == order[0]) | (tallies[sink] == 0), 0, jnp.maximum(slack, 0))
    shifted = jax.random.randint(jax.random.fold_in(own, 4), (amount // 2,), 0, 1 << 20) % (slack + 1)
    tallies = tallies.at[donor].add(-shifted).at[sink].add(shifted)
    labels = jnp.searchsorted(jnp.cumsum(tallies), jnp.arange(rows * top), side="right").astype(jnp.int32)
    grid = labels.reshape(top, rows).T
    grid = grid[jax.random.permutation(jax.random.fold_in(own, 1), rows)]
    offset_by = jax.random.randint(jax.random.fold_in(own, 2), (rows, 1), 0, top)
    return jnp.take_along_axis(grid, (jnp.arange(top)[None, :] + offset_by) % top, axis=1)


def portions_of(amount, total, limit, lean, full):
    portions = [(1 << 20) // math.isqrt(standing ** lean) + 1 for standing in range(1, amount + 1)]
    largest = limit if full else min(limit, max(-(-total // amount), total * portions[0] // sum(portions)))
    least = 1 if total - largest >= amount - 1 else 0
    given, surplus = [largest] + [least] * (amount - 1), total - largest - least * (amount - 1)
    while surplus > 0:
        movable = [i for i in range(1, amount) if given[i] < largest] or [i for i in range(1, amount) if given[i] < limit]
        pool, budget = sum([portions[i] for i in movable]), surplus
        for i in movable:
            addition = min(limit - given[i], max(1, budget * portions[i] // pool), surplus)
            given[i] = given[i] + addition
            surplus = surplus - addition
    return np.array(given)


def centred(rng, dims, spread, bound, cuts=(), kind=jnp.bfloat16):
    drawn = jax.random.normal(rng, dims, jnp.float32) * spread
    if len(cuts) > 0:
        drawn = block_scale(rng, dims, cuts, -0.22, 0.18) * drawn
    return jnp.clip(drawn, min=-bound, max=bound).astype(kind)


def setup_inputs(seed: int = 0) -> dict:
    seeds = jax.random.split(jax.random.key(seed), 13)
    table = centred(seeds[0], (VOCAB, D), 0.7, 5.0, ((0, 32),))
    source_id = draw_source_id(jax.random.fold_in(seeds[12], 71), 0)
    task_mask = draw_task_mask(jax.random.fold_in(seeds[12], 71), 0)
    feature_owner_keys = jax.random.split(jax.random.fold_in(seeds[3], 1), ROWS // ROWS_DEV)
    feature_owner_turns = jax.random.permutation(jax.random.fold_in(seeds[3], 3), ROWS // ROWS_DEV)
    feature_owner = jax.vmap(lambda own, number: routed_block(jax.random.fold_in(seeds[3], 2), own, number, ROWS_DEV, DEVICES, NF, CAP, 2))(feature_owner_keys, feature_owner_turns).reshape((ROWS, NF))
    feature_row = plant(ranked(seeds[4], (ROWS, NF), VOCAB_DEV, 2), jax.random.fold_in(seeds[4], 3), 0, VOCAB_DEV - 1).astype(jnp.int32)
    w_in = centred(seeds[5], (EXPERTS, D, H), D ** -0.5, 0.375)
    b_in = centred(seeds[6], (EXPERTS, H), 0.1, 0.59765625)
    w_out = centred(seeds[7], (EXPERTS, H, D), H ** -0.5, 0.1875)
    b_out = centred(seeds[8], (EXPERTS, D), 0.1, 0.59765625)
    select_weight = centred(seeds[9], (D, NTASK * KSEL * BITS), 0.16, 1.0)
    mix_weight = centred(seeds[10], (D, NTASK * KSEL), 0.03, 0.1796875)
    cotangent = centred(seeds[11], (ROWS, NTASK, D), 1.0, 6.0, ((0, 32),))
    return {"table": table, "source_id": source_id, "task_mask": task_mask, "feature_owner": feature_owner, "feature_row": feature_row, "w_in": w_in, "b_in": b_in, "w_out": w_out, "b_out": b_out, "select_weight": select_weight, "mix_weight": mix_weight, "cotangent": cotangent}


entropy_weight = 0.5
log_guard = 1e-06
smooth_half = 5.0
highest = lax.Precision.HIGHEST

@jax.custom_vjp
def low(v):
    return lax.optimization_barrier(v.astype(jnp.bfloat16)).astype(jnp.float32)

@jax.custom_vjp
def low_back(v):
    return v

def low_keep(v):
    return (low(v), None)

def low_pass(kept, grad):
    return (grad,)

def back_keep(v):
    return (v, None)

def back_low(kept, grad):
    return (low(grad),)
low.defvjp(low_keep, low_pass)
low_back.defvjp(back_keep, back_low)

def smooth_step(values):
    clipped = jnp.clip(values, -smooth_half, smooth_half)
    return -0.002 * clipped * clipped * clipped + 0.15 * clipped + 0.5

def selector_weights(inputs, select_wide, mixer_wide, active):
    row_count = inputs.shape[0]
    logits = jnp.dot(inputs, select_wide, precision=highest).reshape(row_count, NTASK, KSEL, BITS)
    stepped = smooth_step(logits)
    columns = []
    for expert in range(EXPERTS):
        product = jnp.ones((row_count, NTASK, KSEL), jnp.float32)
        for bit_index in range(BITS):
            level_now = stepped[..., bit_index]
            product = product * (level_now if expert >> bit_index & 1 else 1.0 - level_now)
        columns.append(product)
    chosen = jnp.stack(columns, axis=-1)
    mix_logits = jnp.dot(inputs, mixer_wide, precision=highest).reshape(row_count, NTASK, KSEL)
    mixing = jax.nn.softmax(mix_logits, axis=-1)
    gate_mix = lax.optimization_barrier(jnp.sum(mixing[..., None] * chosen, axis=2))
    entropy = -lax.optimization_barrier(jnp.sum(chosen * jnp.log(chosen + log_guard), axis=(2, 3)))
    return (gate_mix, jnp.sum(active * entropy))

def block_forward(inputs, weights, active):
    w_in, b_in, w_out, b_out, select_wide, mixer_wide = weights
    gate_mix, entropy_sum = selector_weights(inputs, select_wide, mixer_wide, active)
    mixed_sum = jnp.zeros((inputs.shape[0], NTASK, D), jnp.float32)
    for expert in range(EXPERTS):
        hidden_pre = low_back(jnp.dot(inputs, w_in[expert], precision=highest)) + b_in[expert]
        hidden = low(jax.nn.silu(hidden_pre))
        result = low_back(jnp.dot(hidden, w_out[expert], precision=highest)) + b_out[expert]
        mixed_sum = mixed_sum + gate_mix[:, :, expert, None] * result[:, None, :]
    return (active[..., None] * mixed_sum, entropy_sum)

def reference(table, source_id, task_mask, feature_owner, feature_row, w_in, b_in, w_out, b_out, select_weight, mix_weight, cotangent):
    active = task_mask[source_id].astype(jnp.float32)
    count = jnp.sum(active)
    weight_rows = jnp.float32(ROWS) / count
    flat_ids = (feature_owner * VOCAB_DEV + feature_row).astype(jnp.int32)

    def lookup(table_wide):
        total = table_wide[flat_ids[:, 0]]
        for feature in range(1, NF):
            total = total + table_wide[flat_ids[:, feature]]
        return total
    summed, lookup_back = jax.vjp(lookup, table.astype(jnp.float32))
    params = tuple((member.astype(jnp.float32) for member in (w_in, b_in, w_out, b_out, select_weight, mix_weight)))
    block_rows = min(ROWS, 4096)
    blocks = ROWS // block_rows

    def one_block(carry, pieces):
        summed_part, active_part, upstream_part = pieces

        def forward(summed_in, *weights):
            return block_forward(low(summed_in), weights, active_part)
        (mixed_part, entropy_part), backward = jax.vjp(forward, summed_part, *params)
        grads = backward((upstream_part.astype(jnp.float32), jnp.float32(entropy_weight)))
        new_carry = tuple((old + new for old, new in zip(carry[:-1], grads[1:]))) + (carry[-1] + entropy_part,)
        return (new_carry, (mixed_part.astype(jnp.bfloat16), grads[0]))
    start = tuple((jnp.zeros_like(member) for member in params)) + (jnp.zeros((), jnp.float32),)
    pieces = (summed.reshape(blocks, block_rows, D), active.reshape(blocks, block_rows, NTASK), cotangent.reshape(blocks, block_rows, NTASK, D))
    totals, (mixed_all, summed_grad) = lax.scan(one_block, start, pieces)
    table_sum, = lookup_back(summed_grad.reshape(ROWS, D))
    mixed = mixed_all.reshape(ROWS, NTASK, D)
    entropy_mean = totals[-1] / count
    return (mixed, weight_rows * table_sum, weight_rows * totals[0], weight_rows * totals[1], weight_rows * totals[2], weight_rows * totals[3], weight_rows * totals[4], weight_rows * totals[5], entropy_mean)
```

```python
import jax
import jax.numpy as jnp
from jax import lax
from jax.experimental import pallas as pl
from jax.experimental.pallas import tpu as pltpu
from jax.sharding import PartitionSpec as P

AXES = ("dp", "outer")
EXPERTS = 4
BITS = 2
KSEL = 4
NTASK = 4
ENTROPY_WEIGHT = 0.5
LOG_GUARD = 1e-06
SMOOTH_HALF = 5.0

F32, BF16, I32 = jnp.float32, jnp.bfloat16, jnp.int32
VMEM = pl.BlockSpec(memory_space=pltpu.VMEM)
NT = (((1,), (1,)), ((), ()))
TN = (((0,), (0,)), ((), ()))
NN = (((1,), (0,)), ((), ()))


def dot(a, b, dims=NN):
    return lax.dot_general(a, b, dims, preferred_element_type=F32)


def iota(shape, axis):
    return lax.broadcasted_iota(I32, shape, axis)


def params(mib):
    return pltpu.CompilerParams(vmem_limit_bytes=mib << 20)


def index_kernel(source_ref, mask_ref, owner_ref, row_ref, send_ref, target_ref, active_ref):
    owners, cap = send_ref.shape[0], send_ref.shape[1] // 2
    rows = owner_ref.shape[1]
    step = 256
    before = (iota((step, step), 0) < iota((step, step), 1)).astype(BF16)
    carry = jnp.zeros((owners, 1), F32)
    high = jnp.zeros((owners, cap), F32)
    low = jnp.zeros((owners, cap), F32)
    for f in range(owner_ref.shape[0]):
        for start in range(0, rows, step):
            owner = owner_ref[f : f + 1, start : start + step]
            row = row_ref[f : f + 1, start : start + step]
            named = (owner == iota((owners, step), 0)).astype(F32)
            named_low = named.astype(BF16)
            earlier = dot(named_low, before) + carry
            carry = carry + jnp.sum(named, axis=1, keepdims=True)
            slot = jnp.sum(named * earlier, axis=0, keepdims=True).astype(I32)
            target_ref[f : f + 1, start : start + step] = owner * cap + slot
            at_slot = (slot == iota((cap, step), 0)).astype(F32).astype(BF16)
            high = high + dot((named * (row >> 8).astype(F32)).astype(BF16), at_slot, NT)
            low = low + dot((named * (row & 255).astype(F32)).astype(BF16), at_slot, NT)
    send_ref[:, :cap] = (high * 256.0 + low).astype(I32)
    sources = mask_ref.shape[1]
    from_source = (source_ref[...] == iota((sources, rows), 0)).astype(F32).astype(BF16)
    active = dot(mask_ref[...].astype(F32).astype(BF16), from_source)
    active_ref[...] = active
    count = jnp.sum(jnp.sum(active, axis=0, keepdims=True), axis=1, keepdims=True)
    send_ref[:, cap:] = jnp.broadcast_to(count, (owners, cap)).astype(I32)


def prepare(source, mask_t, owner_t, row_t, owners, cap):
    rows = owner_t.shape[1]
    return pl.pallas_call(
        index_kernel,
        out_shape=(
            jax.ShapeDtypeStruct((owners, 2 * cap), I32),
            jax.ShapeDtypeStruct(owner_t.shape, I32),
            jax.ShapeDtypeStruct((mask_t.shape[0], rows), F32),
        ),
        in_specs=[VMEM] * 4,
        out_specs=(VMEM,) * 3,
        compiler_params=params(32),
    )(source, mask_t, owner_t, row_t)


def find_kernel(named_ref, table_ref, found_ref):
    lines = named_ref.shape[0]
    slots = found_ref.shape[0]
    per = slots // 128
    first = pl.program_id(0) * per
    blocks = table_ref.shape[0] // 128
    columns = jnp.transpose(named_ref[pl.ds(pl.multiple_of(first, per), per), :].astype(F32), (1, 0))
    parts = []
    for line in range(per):
        column = jnp.broadcast_to(columns[:, line : line + 1], (128, 128)).astype(I32)
        high = (column >> 7).astype(F32).astype(BF16)
        low = ((column & 127) == iota((128, 128), 1)).astype(F32).astype(BF16)
        parts.append((high, low))
    high = jnp.concatenate([p[0] for p in parts], axis=0)
    low = jnp.concatenate([p[1] for p in parts], axis=0)
    zero = jnp.zeros_like(low)
    picks = jnp.concatenate([jnp.where(high == jnp.bfloat16(b), low, zero) for b in range(blocks)], axis=1)
    found_ref[...] = dot(picks, table_ref[...]).astype(BF16)


def find(named, table):
    lines = named.shape[0]
    slots = lines * 128
    step = 1024
    return pl.pallas_call(
        find_kernel,
        grid=(slots // step,),
        out_shape=jax.ShapeDtypeStruct((slots, table.shape[1]), BF16),
        in_specs=[
            pl.BlockSpec(named.shape, lambda i: (0, 0)),
            pl.BlockSpec(table.shape, lambda i: (0, 0)),
        ],
        out_specs=pl.BlockSpec((step, table.shape[1]), lambda i: (i, 0)),
        compiler_params=params(48),
    )(named, table)


def scatter_kernel(scale_ref, named_ref, incoming_ref, sum_ref, pick_ref):
    lines = named_ref.shape[0]
    base = pl.program_id(0) * (sum_ref.shape[0] // 128)
    named = named_ref[...]
    for line in range(lines):
        row = named[line : line + 1, :]
        high = jnp.broadcast_to(row >> 7, (16, 128)).astype(F32).astype(BF16)
        low = ((row & 127) == iota((128, 128), 0)).astype(F32).astype(BF16)
        zero = jnp.zeros_like(low)
        for b in range(sum_ref.shape[0] // 128):
            here = jnp.where(high == (base + b).astype(F32).astype(BF16), jnp.bfloat16(1), jnp.bfloat16(0))
            pick_ref[b * 128 : (b + 1) * 128, line * 128 : (line + 1) * 128] = low * jnp.concatenate([here] * 8, axis=0)
    sum_ref[...] = dot(pick_ref[...], incoming_ref[...]) * scale_ref[0]


def scatter(scale, named, incoming, vocab):
    step = 512
    return pl.pallas_call(
        scatter_kernel,
        grid=(vocab // step,),
        out_shape=jax.ShapeDtypeStruct((vocab, incoming.shape[1]), F32),
        in_specs=[
            pl.BlockSpec(memory_space=pltpu.SMEM),
            pl.BlockSpec(named.shape, lambda i: (0, 0)),
            pl.BlockSpec(incoming.shape, lambda i: (0, 0)),
        ],
        out_specs=pl.BlockSpec((step, incoming.shape[1]), lambda i: (i, 0)),
        scratch_shapes=[pltpu.VMEM((step, named.shape[0] * 128), BF16)],
        compiler_params=params(48),
    )(scale, named, incoming)


def smooth(v):
    c = jnp.clip(v, -SMOOTH_HALF, SMOOTH_HALF)
    return -0.002 * c * c * c + 0.15 * c + 0.5


def smooth_slope(v):
    c = jnp.clip(v, -SMOOTH_HALF, SMOOTH_HALF)
    inside = jnp.where((v >= -SMOOTH_HALF) & (v <= SMOOTH_HALF), 1.0, 0.0)
    return inside * (0.15 - 0.006 * c * c)


def main_kernel(
    scale_ref,
    core_ref,
    target_ref,
    active_ref,
    replied_ref,
    cot_ref,
    w_in_ref,
    b_in_ref,
    w_out_ref,
    b_out_ref,
    gates_ref,
    mixed_ref,
    outgoing_ref,
    keep_ref,
    send_ref,
    small_ref,
    up_ref,
    w_in_sum,
    w_out_sum,
    b_in_sum,
    b_out_sum,
    gates_sum,
    entropy_sum,
    pick_ref,
):
    tile = pl.program_id(0)
    tiles = pl.num_programs(0)
    rows = cot_ref.shape[0] // NTASK
    slots = replied_ref.shape[0]
    blocks = rows // 128
    lines = slots // 128
    zero16 = jnp.bfloat16(0)

    @pl.when(tile == 0)
    def _():
        for ref in (w_in_sum, w_out_sum, b_in_sum, b_out_sum, gates_sum, entropy_sum):
            ref[...] = jnp.zeros_like(ref)

    here = pl.ds(pl.multiple_of(tile * rows, rows), rows)

    target = target_ref[:, here]
    high_low = jnp.concatenate([target >> 7, target & 127, target >> 7, target & 127], axis=0).astype(F32)
    columns = jnp.transpose(high_low, (1, 0))

    def spread(k):
        return jnp.broadcast_to(columns[:, k : k + 1], (rows, 128))

    highs = [spread(f).astype(BF16) for f in range(2)]
    lows = [(spread(2 + f).astype(I32) == iota((rows, 128), 1)).astype(F32).astype(BF16) for f in range(2)]
    picks = []
    for b in range(lines):
        first = jnp.where(highs[0] == jnp.bfloat16(b), lows[0], zero16)
        picks.append(jnp.where(highs[1] == jnp.bfloat16(b), lows[1], first))
    inputs = dot(jnp.concatenate(picks, axis=1), replied_ref[...]).astype(BF16)

    gates_w = gates_ref[...]
    logits = dot(gates_w, inputs, NT)
    active = active_ref[:, here]
    active = jnp.concatenate([active, active], axis=0)

    def group(k):
        return logits[8 * k : 8 * k + 8, :]

    zetas = [[group(j * KSEL + c) for c in range(KSEL)] for j in range(BITS)]
    levels = [[smooth(z) for z in zs] for zs in zetas]
    mix = [group(BITS * KSEL + c) for c in range(KSEL)]
    top = jnp.maximum(jnp.maximum(mix[0], mix[1]), jnp.maximum(mix[2], mix[3]))
    mix = [jnp.exp(m - top) for m in mix]
    total = 1.0 / (mix[0] + mix[1] + mix[2] + mix[3])
    mix = [m * total for m in mix]
    chosen = [
        [
            (levels[0][c] if e & 1 else 1.0 - levels[0][c]) * (levels[1][c] if e & 2 else 1.0 - levels[1][c])
            for e in range(EXPERTS)
        ]
        for c in range(KSEL)
    ]
    gate = [sum(mix[c] * chosen[c][e] for c in range(KSEL)) for e in range(EXPERTS)]
    logs = [[jnp.log(chosen[c][e] + LOG_GUARD) for e in range(EXPERTS)] for c in range(KSEL)]
    entropy = -sum(chosen[c][e] * logs[c][e] for c in range(KSEL) for e in range(EXPERTS))
    entropy_sum[...] += (active * entropy)[:4, :]

    diagonal = (iota((512, 128), 0) >> 2) == iota((512, 128), 1)
    gate_mats = []
    for b in range(blocks):
        mats = []
        for e in range(EXPERTS):
            g = (gate[e] * active)[:, b * 128 : (b + 1) * 128].astype(BF16)
            g = jnp.concatenate([g] * 64, axis=0)
            mats.append(jnp.where(diagonal, g, zero16))
        gate_mats.append(jnp.concatenate(mats, axis=1))
    ups = [dot(gate_mats[b], cot_ref[b * 512 : (b + 1) * 512, :], TN) for b in range(blocks)]

    input_up = jnp.zeros((rows, inputs.shape[1]), F32)
    results = []
    for e in range(EXPERTS):
        result_up = jnp.concatenate([u[e * 128 : (e + 1) * 128, :] for u in ups], axis=0)
        b_out_sum[e : e + 1, :] += jnp.sum(result_up, axis=0, keepdims=True)
        result_low = result_up.astype(BF16)
        pre = dot(inputs, w_in_ref[e]) + b_in_ref[e : e + 1, :].astype(F32)
        logistic = 0.5 * jnp.tanh(0.5 * pre) + 0.5
        hidden = pre * logistic
        slope = logistic + hidden - hidden * logistic
        hidden = hidden.astype(BF16)
        result = dot(hidden, w_out_ref[e]) + b_out_ref[e : e + 1, :].astype(F32)
        results.append(result.astype(BF16))
        hidden_up = dot(result_low, w_out_ref[e], NT) * slope
        b_in_sum[e : e + 1, :] += jnp.sum(hidden_up, axis=0, keepdims=True)
        hidden_low = hidden_up.astype(BF16)
        input_up = input_up + dot(hidden_low, w_in_ref[e], NT)
        w_in_sum[e] += dot(inputs, hidden_low, TN)
        w_out_sum[e] += dot(result_low, hidden, TN)

    gate_up = [[] for _ in range(EXPERTS)]
    for b in range(blocks):
        stacked = jnp.concatenate([r[b * 128 : (b + 1) * 128, :] for r in results], axis=0)
        mixed_ref[b * 512 : (b + 1) * 512, :] = dot(gate_mats[b], stacked).astype(BF16)
        products = dot(cot_ref[b * 512 : (b + 1) * 512, :], stacked, NT)
        for e in range(EXPERTS):
            p = jnp.where(diagonal, products[:, e * 128 : (e + 1) * 128], 0.0)
            p = jnp.sum(p.reshape(64, 8, 128), axis=0)
            gate_up[e].append(p + jnp.concatenate([p[4:], p[:4]], axis=0))
    gate_up = [jnp.concatenate(g, axis=1) * active for g in gate_up]

    level_up = [[None] * KSEL for _ in range(BITS)]
    mixing_up = []
    for c in range(KSEL):
        mixing_up.append(sum(gate_up[e] * chosen[c][e] for e in range(EXPERTS)))
        chosen_up = []
        for e in range(EXPERTS):
            x = chosen[c][e]
            slope_e = logs[c][e] + x / (x + LOG_GUARD)
            chosen_up.append(gate_up[e] * mix[c] - (ENTROPY_WEIGHT * active) * slope_e)
        l0, l1 = levels[0][c], levels[1][c]
        level_up[0][c] = (chosen_up[1] - chosen_up[0]) * (1.0 - l1) + (chosen_up[3] - chosen_up[2]) * l1
        level_up[1][c] = (chosen_up[2] - chosen_up[0]) * (1.0 - l0) + (chosen_up[3] - chosen_up[1]) * l0
    mean_up = sum(mixing_up[c] * mix[c] for c in range(KSEL))
    ups_all = [level_up[j][c] * smooth_slope(zetas[j][c]) for j in range(BITS) for c in range(KSEL)]
    ups_all += [mix[c] * (mixing_up[c] - mean_up) for c in range(KSEL)]
    logits_up = jnp.concatenate(ups_all, axis=0)
    up_high = logits_up.astype(BF16)
    up_low = (logits_up - up_high.astype(F32)).astype(BF16)
    gates_sum[...] += dot(up_high, inputs) + dot(up_low, inputs)
    once = jnp.where((iota(gates_w.shape, 0) & 4) == 0, gates_w, zero16)
    input_up = input_up + dot(up_high, once, TN) + dot(up_low, once, TN)
    up_ref[here, :] = input_up.astype(BF16)

    @pl.when(tile == tiles - 1)
    def _():
        scale = scale_ref[0]
        parts = 4
        for e in range(EXPERTS):
            first = (w_in_sum[e] * scale).astype(BF16)
            second = (w_out_sum[e] * scale).astype(BF16)

            @pl.when(core_ref[0] == 0)
            def _():
                keep_ref[e] = first
                send_ref[e] = second

            @pl.when(core_ref[0] != 0)
            def _():
                keep_ref[e] = second
                send_ref[e] = first

        for k in range(12):
            small_ref[4 * k : 4 * k + 4, :] = gates_sum[8 * k : 8 * k + 4, :] * scale
        width = small_ref.shape[1]
        for q in range(parts):
            small_ref[48 + 4 * q : 52 + 4 * q, :] = b_in_sum[:, q * width : (q + 1) * width] * scale
        small_ref[64:68, :] = b_out_sum[...] * scale
        entropy_all = jnp.sum(jnp.sum(entropy_sum[...], axis=0, keepdims=True), axis=1, keepdims=True)
        small_ref[68:72, :] = jnp.broadcast_to(entropy_all, (4, width))

        all_rows = up_ref.shape[0]

        def fill(step, carry):
            per = pick_ref.shape[0] // 128
            for piece in range(all_rows // 128):
                lanes = slice(piece * 128, (piece + 1) * 128)
                named = target_ref[:, lanes]
                high = [jnp.broadcast_to(named[f : f + 1, :] >> 7, (16, 128)).astype(F32).astype(BF16) for f in range(2)]
                low = [((named[f : f + 1, :] & 127) == iota((128, 128), 0)).astype(F32).astype(BF16) for f in range(2)]
                for b in range(per):
                    line = (step * per + b).astype(F32).astype(BF16)
                    at = [
                        jnp.concatenate([jnp.where(h == line, jnp.bfloat16(1), zero16)] * 8, axis=0) for h in high
                    ]
                    pick_ref[b * 128 : (b + 1) * 128, lanes] = low[0] * at[0] + low[1] * at[1]
            count = pick_ref.shape[0]
            out = pl.ds(pl.multiple_of(step * count, count), count)
            outgoing_ref[out, :] = dot(pick_ref[...], up_ref[...]).astype(BF16)
            return carry

        lax.fori_loop(0, outgoing_ref.shape[0] // pick_ref.shape[0], fill, 0)


def experts(scale, core, target, active, replied, cot, w_in, b_in, w_out, b_out, gates):
    rows, slots = target.shape[1], replied.shape[0]
    width, hidden = w_in.shape[1], w_in.shape[2]
    step = 256
    whole = lambda a: pl.BlockSpec(a.shape, lambda i: (0,) * a.ndim)
    smem = pl.BlockSpec(memory_space=pltpu.SMEM)
    grads = jax.ShapeDtypeStruct((EXPERTS, width, hidden), BF16)
    whole_out = lambda shape: pl.BlockSpec(shape, lambda i: (0,) * len(shape))
    return pl.pallas_call(
        main_kernel,
        grid=(rows // step,),
        out_shape=(
            jax.ShapeDtypeStruct(cot.shape, BF16),
            jax.ShapeDtypeStruct((slots, width), BF16),
            grads,
            grads,
            jax.ShapeDtypeStruct((72, width), F32),
        ),
        in_specs=[smem, smem, whole(target), whole(active), whole(replied)]
        + [pl.BlockSpec((step * NTASK, width), lambda i: (i, 0))]
        + [whole(a) for a in (w_in, b_in, w_out, b_out, gates)],
        out_specs=(
            pl.BlockSpec((step * NTASK, width), lambda i: (i, 0)),
            whole_out((slots, width)),
            whole_out(grads.shape),
            whole_out(grads.shape),
            whole_out((72, width)),
        ),
        scratch_shapes=[
            pltpu.VMEM((rows, width), BF16),
            pltpu.VMEM((EXPERTS, width, hidden), F32),
            pltpu.VMEM((EXPERTS, width, hidden), F32),
            pltpu.VMEM((EXPERTS, hidden), F32),
            pltpu.VMEM((EXPERTS, width), F32),
            pltpu.VMEM((96, width), F32),
            pltpu.VMEM((4, step), F32),
            pltpu.VMEM((512, rows), BF16),
        ],
        compiler_params=params(58),
    )(scale, core, target, active, replied, cot, w_in, b_in, w_out, b_out, gates)


def swap(x, mask, devices):
    return lax.ppermute(x, AXES, [(i, i ^ mask) for i in range(devices)])


def bits_of(count):
    return range(count.bit_length() - 1)


def sum_over_devices(x, devices):
    for k in bits_of(devices):
        x = x + swap(x, 1 << k, devices)
    return x


def halves(x, bit):
    rows = x.shape[0] // 2
    keep = lax.dynamic_slice_in_dim(x, bit * rows, rows, 0)
    give = lax.dynamic_slice_in_dim(x, (1 - bit) * rows, rows, 0)
    return keep, give.astype(BF16)


def joined(mine, other, bit):
    return jnp.where(bit == 0, jnp.concatenate([mine, other]), jnp.concatenate([other, mine]))


def sum_weights(keep, send, index, dp_count, outer_count):
    devices = dp_count * outer_count
    core = outer_count
    outer = [1 << k for k in bits_of(outer_count)]
    across = [outer_count << k for k in bits_of(dp_count)][1:]
    first = [outer[0], across[0]]
    rest = outer[1:] + across[1:]

    def bit(mask):
        return (index // mask) % 2

    experts, width, hidden = keep.shape
    whole = keep.astype(F32) + swap(send, core, devices).astype(F32)
    parts = [whole[: experts // 2], whole[experts // 2 :]]
    parts = [p.reshape(experts // 2 * width, hidden) for p in parts]
    for orders in (first, first[::-1]):
        split = [halves(p, bit(m)) for p, m in zip(parts, orders)]
        parts = [k + swap(g, m, devices).astype(F32) for (k, g), m in zip(split, orders)]
    both = jnp.stack(parts, axis=1)
    for mask in rest:
        k, g = halves(both, bit(mask))
        both = k + swap(g, mask, devices).astype(F32)
    both = both.astype(BF16)
    for mask in rest[::-1]:
        both = joined(both, swap(both, mask, devices), bit(mask))
    parts = [both[:, 0], both[:, 1]]
    for orders in (first[::-1], first):
        parts = [joined(p, swap(p, m, devices), bit(m)) for p, m in zip(parts, orders)]
    mine = jnp.concatenate(parts).reshape(experts, width, hidden)
    other = swap(mine, core, devices)
    at_zero = bit(core) == 0
    return jnp.where(at_zero, mine, other).astype(F32), jnp.where(at_zero, other, mine).astype(F32)


def on_device(
    table,
    source_id,
    task_mask,
    feature_owner,
    feature_row,
    w_in,
    b_in,
    w_out,
    b_out,
    select_weight,
    mix_weight,
    cotangent,
):
    rows = source_id.shape[0]
    dp_count, outer_count = lax.axis_size("dp"), lax.axis_size("outer")
    devices = dp_count * outer_count
    index = lax.axis_index("dp") * outer_count + lax.axis_index("outer")
    vocab, width = table.shape
    per_row = feature_owner.shape[1]
    cap = 2 * per_row * rows // devices
    slots = devices * cap

    def exchange(x):
        return lax.all_to_all(x, AXES, split_axis=0, concat_axis=0, tiled=True)

    request, target, active = prepare(
        source_id.reshape(1, rows), task_mask.T, feature_owner.T, feature_row.T, devices, cap
    )
    arrived = exchange(request)
    named = arrived[:, :cap].reshape(slots // 128, 128)
    weight_rows = (jnp.float32(rows * devices) / jnp.sum(arrived[:, cap]).astype(F32)).reshape(1)
    found = find(named, table)
    replied = exchange(found.reshape(devices, cap, width)).reshape(slots, width)

    select = select_weight.T.reshape(NTASK, KSEL, BITS, width).transpose(2, 1, 0, 3)
    mix = mix_weight.T.reshape(NTASK, KSEL, width).transpose(1, 0, 2)
    gates = jnp.concatenate([select.reshape(BITS * KSEL, NTASK, width), mix])
    gates = jnp.concatenate([gates, gates], axis=1).reshape(-1, width)
    core = (index // outer_count) % 2
    mixed, outgoing, keep, send, small = experts(
        weight_rows,
        core.reshape(1).astype(I32),
        target,
        active,
        replied,
        cotangent.reshape(rows * NTASK, width),
        w_in,
        b_in,
        w_out,
        b_out,
        gates,
    )
    incoming = exchange(outgoing.reshape(devices, cap, width)).reshape(slots, width)
    w_in_sum, w_out_sum = sum_weights(keep, send, index, dp_count, outer_count)
    small = sum_over_devices(small, devices)
    table_sum = scatter(weight_rows, named, incoming, vocab)
    select_sum = small[:32].reshape(BITS, KSEL, NTASK, width).transpose(2, 1, 0, 3).reshape(32, width).T
    mix_sum = small[32:48].reshape(KSEL, NTASK, width).transpose(1, 0, 2).reshape(16, width).T
    b_in_sum = small[48:64].reshape(4, EXPERTS, width).transpose(1, 0, 2).reshape(EXPERTS, -1)
    entropy_mean = small[68, 0] * weight_rows[0] / (rows * devices)
    return (
        mixed.reshape(rows, NTASK, width),
        table_sum,
        w_in_sum,
        b_in_sum,
        w_out_sum.transpose(0, 2, 1),
        small[64:68],
        select_sum,
        mix_sum,
        entropy_mean,
    )


def solution(mesh):
    rows = P(AXES)
    flat = P(AXES, None)
    cube = P(AXES, None, None)
    placed = (flat, rows, P(), flat, flat, P(), P(), P(), P(), P(), P(), cube)
    return jax.shard_map(
        on_device,
        mesh=mesh,
        in_specs=placed,
        out_specs=(cube, flat, P(), P(), P(), P(), P(), P(), P()),
        check_vma=False,
    )
```

```python
import jax
import jax.numpy as jnp
from jax import lax
from jax.experimental import pallas as pl
from jax.experimental.pallas import tpu as pltpu
from jax.sharding import PartitionSpec as P

AXES = ("dp", "outer")
EXPERTS = 4
BITS = 2
KSEL = 4
NTASK = 4
ENTROPY_WEIGHT = 0.5
LOG_GUARD = 1e-06
SMOOTH_HALF = 5.0
SMALL = 11

F32, BF16, I32 = jnp.float32, jnp.bfloat16, jnp.int32
VMEM = pl.BlockSpec(memory_space=pltpu.VMEM)
HBM = pl.BlockSpec(memory_space=pl.ANY)
NT = (((1,), (1,)), ((), ()))
TN = (((0,), (0,)), ((), ()))
NN = (((1,), (0,)), ((), ()))


def dot(a, b, dims=NN):
    return lax.dot_general(a, b, dims, preferred_element_type=F32)


def iota(shape, axis):
    return lax.broadcasted_iota(I32, shape, axis)


def params(mib):
    return pltpu.CompilerParams(vmem_limit_bytes=mib << 20)


def index_kernel(*refs):
    given, (send_ref, target_ref, active_ref), held, sem = refs[:4], refs[4:7], refs[7:11], refs[11]
    copies = [pltpu.make_async_copy(g, h, sem.at[k]) for k, (g, h) in enumerate(zip(given, held))]
    for copy in copies:
        copy.start()
    for copy in copies:
        copy.wait()
    source_ref, mask_ref, owner_ref, row_ref = held
    owners, cap = send_ref.shape[0], send_ref.shape[1] // 2
    rows = owner_ref.shape[1]
    step = 256
    before = (iota((step, step), 0) < iota((step, step), 1)).astype(BF16)
    carry = jnp.zeros((owners, 1), F32)
    high = jnp.zeros((owners, cap), F32)
    low = jnp.zeros((owners, cap), F32)
    for f in range(owner_ref.shape[0]):
        for start in range(0, rows, step):
            owner = owner_ref[f : f + 1, start : start + step]
            row = row_ref[f : f + 1, start : start + step]
            named = (owner == iota((owners, step), 0)).astype(F32)
            named_low = named.astype(BF16)
            earlier = dot(named_low, before) + carry
            carry = carry + jnp.sum(named, axis=1, keepdims=True)
            slot = jnp.sum(named * earlier, axis=0, keepdims=True).astype(I32)
            target_ref[f : f + 1, start : start + step] = owner * cap + slot
            at_slot = (slot == iota((cap, step), 0)).astype(F32).astype(BF16)
            high = high + dot((named * (row >> 8).astype(F32)).astype(BF16), at_slot, NT)
            low = low + dot((named * (row & 255).astype(F32)).astype(BF16), at_slot, NT)
    send_ref[:, :cap] = (high * 256.0 + low).astype(I32)
    sources = mask_ref.shape[1]
    from_source = (source_ref[...] == iota((sources, rows), 0)).astype(F32).astype(BF16)
    active = dot(mask_ref[...].astype(F32).astype(BF16), from_source)
    active_ref[...] = active
    count = jnp.sum(jnp.sum(active, axis=0, keepdims=True), axis=1, keepdims=True)
    send_ref[:, cap:] = jnp.broadcast_to(count, (owners, cap)).astype(I32)


def prepare(source, mask_t, owner_t, row_t, owners, cap):
    rows = owner_t.shape[1]
    return pl.pallas_call(
        index_kernel,
        out_shape=(
            jax.ShapeDtypeStruct((owners, 2 * cap), I32),
            jax.ShapeDtypeStruct(owner_t.shape, I32),
            jax.ShapeDtypeStruct((mask_t.shape[0], rows), F32),
        ),
        in_specs=[HBM] * 4,
        out_specs=(VMEM,) * 3,
        scratch_shapes=[pltpu.VMEM(x.shape, I32) for x in (source, mask_t, owner_t, row_t)]
        + [pltpu.SemaphoreType.DMA((4,))],
        compiler_params=params(60),
    )(source, mask_t, owner_t, row_t)


def find_kernel(named_ref, table_ref, found_ref):
    slots = found_ref.shape[0]
    per = slots // 128
    first = pl.program_id(0) * per
    blocks = table_ref.shape[0] // 128
    columns = jnp.transpose(named_ref[pl.ds(pl.multiple_of(first, per), per), :].astype(F32), (1, 0))
    parts = []
    for line in range(per):
        column = jnp.broadcast_to(columns[:, line : line + 1], (128, 128)).astype(I32)
        high = (column >> 7).astype(F32).astype(BF16)
        low = ((column & 127) == iota((128, 128), 1)).astype(F32).astype(BF16)
        parts.append((high, low))
    high = jnp.concatenate([p[0] for p in parts], axis=0)
    low = jnp.concatenate([p[1] for p in parts], axis=0)
    zero = jnp.zeros_like(low)
    picks = jnp.concatenate([jnp.where(high == jnp.bfloat16(b), low, zero) for b in range(blocks)], axis=1)
    found_ref[...] = dot(picks, table_ref[...]).astype(BF16)


def find(named, table):
    lines = named.shape[0]
    slots = lines * 128
    step = 1024
    return pl.pallas_call(
        find_kernel,
        grid=(slots // step,),
        out_shape=jax.ShapeDtypeStruct((slots, table.shape[1]), BF16),
        in_specs=[
            pl.BlockSpec(named.shape, lambda i: (0, 0)),
            pl.BlockSpec(table.shape, lambda i: (0, 0)),
        ],
        out_specs=pl.BlockSpec((step, table.shape[1]), lambda i: (i, 0)),
        compiler_params=params(48),
    )(named, table)


def scatter_kernel(scale_ref, named_ref, incoming_ref, sum_ref, pick_ref):
    count = sum_ref.shape[0] // 128
    base = pl.program_id(0) * count
    pieces = 4
    lines = named_ref.shape[0] // pieces
    zero, one = jnp.bfloat16(0), jnp.bfloat16(1)

    def build(q):
        for line in range(q * lines, (q + 1) * lines):
            row = named_ref[line : line + 1, :]
            high = jnp.broadcast_to(row >> 7, (16, 128)).astype(F32).astype(BF16)
            low = ((row & 127) == iota((128, 128), 0)).astype(F32).astype(BF16).reshape(8, 16, 128)
            for b in range(count):
                here = jnp.where(high == (base + b).astype(F32).astype(BF16), one, zero)[None]
                pick_ref[b * 128 : (b + 1) * 128, line * 128 : (line + 1) * 128] = (low * here).reshape(128, 128)

    build(0)
    total = jnp.zeros(sum_ref.shape, F32)
    for q in range(pieces):
        if q + 1 < pieces:
            build(q + 1)
        at = slice(q * lines * 128, (q + 1) * lines * 128)
        total = total + dot(pick_ref[:, at], incoming_ref[at, :])
    sum_ref[...] = total * scale_ref[0]


def scatter(scale, named, incoming, vocab):
    step = 1024
    width = incoming.shape[1]
    return pl.pallas_call(
        scatter_kernel,
        grid=(vocab // step,),
        out_shape=jax.ShapeDtypeStruct((vocab, width), F32),
        in_specs=[
            pl.BlockSpec(memory_space=pltpu.SMEM),
            pl.BlockSpec(named.shape, lambda i: (0, 0)),
            pl.BlockSpec(incoming.shape, lambda i: (0, 0)),
        ],
        out_specs=pl.BlockSpec((step, width), lambda i: (i, 0)),
        scratch_shapes=[pltpu.VMEM((step, named.shape[0] * 128), BF16)],
        compiler_params=params(48),
    )(scale, named, incoming)


def smooth(v):
    c = jnp.clip(v, -SMOOTH_HALF, SMOOTH_HALF)
    return -0.002 * c * c * c + 0.15 * c + 0.5


def smooth_slope(v):
    c = jnp.clip(v, -SMOOTH_HALF, SMOOTH_HALF)
    inside = jnp.where((v >= -SMOOTH_HALF) & (v <= SMOOTH_HALF), 1.0, 0.0)
    return inside * (0.15 - 0.006 * c * c)


def main_kernel(
    scale_ref,
    core_ref,
    active_ref,
    b_in_ref,
    b_out_ref,
    gates_ref,
    target_ref,
    replied_hbm,
    cot_hbm,
    w_in_hbm,
    w_out_hbm,
    keep_in_hbm,
    keep_out_hbm,
    send_in_hbm,
    send_out_hbm,
    outgoing_hbm,
    mixed_hbm,
    small_ref,
    outgoing_ref,
    mixed_ref,
    fill_ref,
    pick_ref,
    replied_ref,
    cot_ref,
    w_in_ref,
    w_out_ref,
    result_ref,
    hidden_ref,
    hidden_up_ref,
    w_in_low,
    w_out_low,
    b_in_sum,
    b_out_sum,
    in_sem,
    out_sem,
):
    rows = active_ref.shape[1]
    part = 64
    blocks = rows // part
    flat = part * NTASK
    slots, width = replied_ref.shape
    hidden_width = w_in_ref.shape[2]
    chunk = 256
    chunks = hidden_width // chunk
    half = EXPERTS // 2
    zero16 = jnp.bfloat16(0)

    loads = {}

    def load(name, source, target):
        loads[name] = pltpu.make_async_copy(source, target, in_sem.at[len(loads)])
        loads[name].start()

    def loaded(name):
        if name in loads:
            loads.pop(name).wait()

    load("replied", replied_hbm, replied_ref)
    load(("in", 0), w_in_hbm.at[0], w_in_ref.at[0])
    load("cot", cot_hbm, cot_ref)
    load(("out", 0), w_out_hbm.at[0], w_out_ref.at[0])
    for e in range(1, EXPERTS):
        load(("in", e), w_in_hbm.at[e], w_in_ref.at[e])
        load(("out", e), w_out_hbm.at[e], w_out_ref.at[e])

    stores = []

    def store(source, target):
        stores.append(pltpu.make_async_copy(source, target, out_sem.at[len(stores)]))
        stores[-1].start()

    target = target_ref[...]
    columns = jnp.transpose(jnp.concatenate([target >> 7, target & 127] * 2, axis=0).astype(F32), (1, 0))

    def spread(k):
        return jnp.broadcast_to(columns[:, k : k + 1], (rows, 128))

    highs = [spread(f).astype(BF16) for f in range(2)]
    lows = [(spread(2 + f).astype(I32) == iota((rows, 128), 1)).astype(F32).astype(BF16) for f in range(2)]
    pieces = 4
    lines = slots // 128 // pieces

    def pick(p):
        for b in range(p * lines, (p + 1) * lines):
            first = jnp.where(highs[0] == jnp.bfloat16(b), lows[0], zero16)
            pick_ref[:, b * 128 : (b + 1) * 128] = jnp.where(highs[1] == jnp.bfloat16(b), lows[1], first)

    pick(0)
    loaded("replied")
    inputs = jnp.zeros((rows, width), F32)
    for p in range(pieces):
        if p + 1 < pieces:
            pick(p + 1)
        at = slice(p * lines * 128, (p + 1) * lines * 128)
        inputs = inputs + dot(pick_ref[:, at], replied_ref[at, :])
    inputs = inputs.astype(BF16)
    inputs_t = jnp.transpose(inputs, (1, 0))

    gates_w = gates_ref[...]
    once = jnp.where((iota(gates_w.shape, 0) & 4) == 0, gates_w, zero16)
    logits = dot(gates_w, inputs, NT)
    active = active_ref[...]
    active = jnp.concatenate([active, active], axis=0)
    along = iota((part, flat), 0) == (iota((part, flat), 1) >> 2)
    repeat = along.astype(F32).astype(BF16)
    own_task = iota((8, flat), 0) == (iota((8, flat), 1) & 3)

    def group(k):
        return logits[8 * k : 8 * k + 8, :]

    zetas = [[group(n * KSEL + c) for c in range(KSEL)] for n in range(BITS)]
    levels = [[smooth(z) for z in zs] for zs in zetas]
    mix = [group(BITS * KSEL + c) for c in range(KSEL)]
    top = jnp.maximum(jnp.maximum(mix[0], mix[1]), jnp.maximum(mix[2], mix[3]))
    mix = [jnp.exp(m - top) for m in mix]
    total = 1.0 / (mix[0] + mix[1] + mix[2] + mix[3])
    mix = [m * total for m in mix]
    chosen = [
        [
            (levels[0][c] if e & 1 else 1.0 - levels[0][c]) * (levels[1][c] if e & 2 else 1.0 - levels[1][c])
            for e in range(EXPERTS)
        ]
        for c in range(KSEL)
    ]
    gate = [sum(mix[c] * chosen[c][e] for c in range(KSEL)) * active for e in range(EXPERTS)]

    loaded("cot")
    ups, gate_rows = [], []
    for b in range(blocks):
        g = [x[:, b * part : (b + 1) * part] for x in gate]
        gate_rows.append(jnp.concatenate(g, axis=1).astype(BF16))
        wide = dot(jnp.concatenate(g, axis=0).astype(BF16), repeat)
        mats = []
        for e in range(EXPERTS):
            row = jnp.sum(jnp.where(own_task, wide[8 * e : 8 * e + 8, :], 0.0), axis=0, keepdims=True)
            row = jnp.broadcast_to(row, (part, flat)).astype(BF16)
            mats.append(jnp.where(along, row, zero16))
        cot = cot_ref[b * part : (b + 1) * part].reshape(flat, width)
        ups.append(dot(jnp.concatenate(mats, axis=0), cot))
    result_up = [jnp.concatenate([u[e * part : (e + 1) * part, :] for u in ups], axis=0) for e in range(EXPERTS)]
    result_low = [u.astype(BF16) for u in result_up]

    def into_tiles(low, e, part):
        part = part * scale_ref[0]
        per = width // 16
        for q in range(hidden_width // 128):
            low[e, q * per : (q + 1) * per] = part[:, q * 128 : (q + 1) * 128].astype(BF16).reshape(per, 16, 128)

    def first_layer(e, c):
        loaded(("in", e))
        loaded(("out", e))
        at = slice(c * chunk, (c + 1) * chunk)
        pre = dot(inputs, w_in_ref[e, :, at]) + b_in_ref[e : e + 1, at].astype(F32)
        logistic = 0.5 * jnp.tanh(0.5 * pre) + 0.5
        hidden = pre * logistic
        slope = logistic + hidden - hidden * logistic
        hidden_ref[e % 2, :, at] = hidden.astype(BF16)
        hidden_up = dot(result_low[e], w_out_ref[e, at, :], NT) * slope
        b_in_sum[e : e + 1, at] = jnp.sum(hidden_up, axis=0, keepdims=True)
        hidden_up_ref[e % 2, :, at] = hidden_up.astype(BF16)

    input_up = jnp.zeros((rows, width), F32)

    def second_layer(e, c):
        nonlocal input_up
        if c == 0:
            result = dot(hidden_ref[e % 2], w_out_ref[e]) + b_out_ref[e : e + 1, :].astype(F32)
            result = result.astype(BF16)
            result_ref[:, e] = result.reshape(blocks, part, width)
            b_out_sum[e : e + 1, :] = jnp.sum(result_up[e], axis=0, keepdims=True)
        elif c == 1:
            input_up = input_up + dot(hidden_up_ref[e % 2], w_in_ref[e], NT)
        elif c == 2:
            into_tiles(w_in_low, e, dot(inputs_t, hidden_up_ref[e % 2]))
        else:
            into_tiles(w_out_low, e, dot(jnp.transpose(result_low[e], (1, 0)), hidden_ref[e % 2]))

    wide_rows = rows // 128
    at_high, at_low = [], []
    for piece in range(wide_rows):
        at = target[:, piece * 128 : (piece + 1) * 128]
        at_high.append([jnp.broadcast_to(at[f : f + 1, :] >> 7, (16, 128)).astype(F32).astype(BF16) for f in range(2)])
        low = [(at[f : f + 1, :] & 127) == iota((128, 128), 0) for f in range(2)]
        at_low.append([x.astype(F32).astype(BF16).reshape(8, 16, 128) for x in low])

    def fill(line):
        for piece in range(wide_rows):
            here = [jnp.where(h == jnp.bfloat16(line), jnp.bfloat16(1), zero16)[None] for h in at_high[piece]]
            fill_ref[line * 128 : (line + 1) * 128, piece * 128 : (piece + 1) * 128] = (
                at_low[piece][0] * here[0] + at_low[piece][1] * here[1]
            ).reshape(128, 128)

    for c in range(chunks):
        first_layer(0, c)
    line = 0
    for e in range(EXPERTS):
        for c in range(chunks):
            if e + 1 < EXPERTS:
                first_layer(e + 1, c)
            second_layer(e, c)
            for _ in range(slots // 128 // (EXPERTS * chunks)):
                fill(line)
                line += 1

    core = core_ref[0]
    for i in range(half):
        mine = core * half + i
        other = (1 - core) * half + i
        store(w_in_low.at[mine], keep_in_hbm.at[i])
        store(w_out_low.at[mine], keep_out_hbm.at[i])
        store(w_in_low.at[other], send_in_hbm.at[i])
        store(w_out_low.at[other], send_out_hbm.at[i])

    down = (iota((flat, flat), 0) >> 2) == (iota((flat, flat), 1) & (part - 1))
    gate_up = [[] for _ in range(EXPERTS)]
    for b in range(blocks):
        cot = cot_ref[b * part : (b + 1) * part].reshape(flat, width)
        products = jnp.where(down, dot(cot, result_ref[b].reshape(flat, width), NT), 0.0)
        p = jnp.sum(products.reshape(flat // 8, 8, flat), axis=0)
        p = p + jnp.concatenate([p[4:], p[:4]], axis=0)
        for e in range(EXPERTS):
            gate_up[e].append(p[:, e * part : (e + 1) * part])
    gate_up = [jnp.concatenate(g, axis=1) * active for g in gate_up]
    level_up = [[None] * KSEL for _ in range(BITS)]
    mixing_up = []
    entropy = 0.0
    for c in range(KSEL):
        mixing_up.append(sum(gate_up[e] * chosen[c][e] for e in range(EXPERTS)))
        chosen_up = []
        for e in range(EXPERTS):
            x = chosen[c][e]
            log = jnp.log(x + LOG_GUARD)
            entropy = entropy - x * log
            chosen_up.append(gate_up[e] * mix[c] - (ENTROPY_WEIGHT * active) * (log + x / (x + LOG_GUARD)))
        l0, l1 = levels[0][c], levels[1][c]
        level_up[0][c] = (chosen_up[1] - chosen_up[0]) * (1.0 - l1) + (chosen_up[3] - chosen_up[2]) * l1
        level_up[1][c] = (chosen_up[2] - chosen_up[0]) * (1.0 - l0) + (chosen_up[3] - chosen_up[1]) * l0
    entropy = (active * entropy)[:4, :]
    mean_up = sum(mixing_up[c] * mix[c] for c in range(KSEL))
    ups_all = [level_up[n][c] * smooth_slope(zetas[n][c]) for n in range(BITS) for c in range(KSEL)]
    ups_all += [mix[c] * (mixing_up[c] - mean_up) for c in range(KSEL)]
    logits_up = jnp.concatenate(ups_all, axis=0)
    up_high = logits_up.astype(BF16)
    up_low = (logits_up - up_high.astype(F32)).astype(BF16)
    input_up = (input_up + dot(up_high, once, TN) + dot(up_low, once, TN)).astype(BF16)
    for b in range(blocks):
        mats = jnp.where(down, jnp.concatenate([gate_rows[b]] * (flat // 8), axis=0), zero16)
        mixed = dot(mats, result_ref[b].reshape(flat, width))
        mixed_ref[b * part : (b + 1) * part] = mixed.reshape(part, NTASK, width).astype(BF16)
    store(mixed_ref, mixed_hbm)
    span = slots // pieces
    for p in range(pieces):
        at = pl.ds(p * span, span)
        outgoing_ref[at, :] = dot(fill_ref[at, :], input_up).astype(BF16)
        store(outgoing_ref.at[at], outgoing_hbm.at[at])

    scale = scale_ref[0]
    gates_sum = (dot(up_high, inputs) + dot(up_low, inputs)) * scale
    small_ref[...] = jnp.zeros_like(small_ref)
    n = 0

    def put(values):
        nonlocal n
        for q in range(values.shape[1] // 128):
            small_ref[n // 4, n % 4 * 4 : n % 4 * 4 + 4, :] = values[:, q * 128 : (q + 1) * 128]
            n += 1

    for k in range(12):
        put(gates_sum[8 * k : 8 * k + 4, :])
    put(b_out_sum[...] * scale)
    put(b_in_sum[...] * scale)
    put(entropy)
    for copy in stores:
        copy.wait()


def experts(scale, core, active, target, replied, cot, w_in, b_in, w_out, b_out, gates):
    rows, slots = active.shape[1], replied.shape[0]
    width, hidden = w_in.shape[1], w_in.shape[2]
    smem = pl.BlockSpec(memory_space=pltpu.SMEM)
    hbm = pl.BlockSpec(memory_space=pl.ANY)
    grads = jax.ShapeDtypeStruct((EXPERTS // 2, width * hidden // 2048, 16, 128), BF16)
    low = pltpu.VMEM((EXPERTS,) + grads.shape[1:], BF16)
    act = pltpu.VMEM((2, rows, hidden), BF16)
    result = (rows // 64, EXPERTS, 64, width)
    return pl.pallas_call(
        main_kernel,
        out_shape=(
            grads,
            grads,
            grads,
            grads,
            jax.ShapeDtypeStruct((slots, width), BF16),
            jax.ShapeDtypeStruct(cot.shape, BF16),
            jax.ShapeDtypeStruct((SMALL, 16, 128), F32),
        ),
        in_specs=[smem, smem] + [VMEM] * 5 + [hbm] * 4,
        out_specs=(hbm,) * 6 + (VMEM,),
        scratch_shapes=[
            pltpu.VMEM((slots, width), BF16),
            pltpu.VMEM(cot.shape, BF16),
            pltpu.VMEM((slots, rows), BF16),
            pltpu.VMEM((rows, slots), BF16),
            pltpu.VMEM(replied.shape, BF16),
            pltpu.VMEM(cot.shape, BF16),
            pltpu.VMEM(w_in.shape, BF16),
            pltpu.VMEM(w_out.shape, BF16),
            pltpu.VMEM(result, BF16),
            act,
            act,
            low,
            low,
            pltpu.VMEM((EXPERTS, hidden), F32),
            pltpu.VMEM((EXPERTS, width), F32),
            pltpu.SemaphoreType.DMA((2 + 2 * EXPERTS,)),
            pltpu.SemaphoreType.DMA((4 * EXPERTS // 2 + 5,)),
        ],
        compiler_params=params(60),
    )(scale, core, active, b_in, b_out, gates, target, replied, cot, w_in, w_out)


def swap(x, mask, devices):
    return lax.ppermute(x, AXES, [(i, i ^ mask) for i in range(devices)])


def bits_of(count):
    return range(count.bit_length() - 1)


def sum_over_devices(x, devices):
    for k in bits_of(devices):
        x = x + swap(x, 1 << k, devices)
    return x


def halves(x, bit):
    rows = x.shape[0] // 2
    keep = lax.dynamic_slice_in_dim(x, bit * rows, rows, 0)
    give = lax.dynamic_slice_in_dim(x, (1 - bit) * rows, rows, 0)
    return keep, give.astype(BF16)


def joined(mine, other, bit):
    return jnp.where(bit == 0, jnp.concatenate([mine, other]), jnp.concatenate([other, mine]))


def tied(*values):
    return lax.optimization_barrier(values)


def sum_weights(keeps, sends, small, incoming, index, dp_count, outer_count):
    devices = dp_count * outer_count
    core = outer_count
    outer = [1 << k for k in bits_of(outer_count)]
    across = [outer_count << k for k in bits_of(dp_count)][1:]
    first = [outer[0], across[0]]
    rest = outer[1:] + across[1:]

    def bit(mask):
        return (index // mask) % 2

    share = -(-small.shape[0] // devices) * devices // 2
    small = jnp.pad(small, ((0, 2 * share - small.shape[0]), (0, 0), (0, 0)))
    mine, others = halves(small, bit(core))
    tiles = keeps[0].shape[1]
    got = [swap(send, core, devices) for send in sends] + [swap(others, core, devices)]
    pieces = [[k for k in keep.astype(F32) + g.astype(F32)] for keep, g in zip(keeps, got)]
    pieces[0][0] = jnp.concatenate([pieces[0][0], mine + got[-1].astype(F32)])
    for orders in (first, first[::-1]):
        for n, parts in enumerate(pieces):
            split = [halves(p, bit(m)) for p, m in zip(parts, orders)]
            pieces[n] = [k + swap(g, m, devices).astype(F32) for (k, g), m in zip(split, orders)]
    for mask in rest:
        for n, parts in enumerate(pieces):
            split = [halves(p, bit(mask)) for p in parts]
            cut = split[0][0].shape[0]
            got = swap(jnp.concatenate([g for _, g in split]), mask, devices).astype(F32)
            pieces[n] = [split[0][0] + got[:cut], split[1][0] + got[cut:]]
    pieces = [[p.astype(BF16) for p in parts] for parts in pieces]
    for mask in rest[::-1]:
        for n, parts in enumerate(pieces):
            cut = parts[0].shape[0]
            got = swap(jnp.concatenate(parts), mask, devices)
            pieces[n] = [joined(parts[0], got[:cut], bit(mask)), joined(parts[1], got[cut:], bit(mask))]
    for step, orders in enumerate((first[::-1], first)):
        pieces = [[joined(p, swap(p, m, devices), bit(m)) for p, m in zip(parts, orders)] for parts in pieces]
        if step == 0:
            pieces, incoming = tied(pieces, incoming)
    small = pieces[0][0][tiles:]
    small = joined(small, swap(small, core, devices), bit(core)).astype(F32)
    pieces[0][0] = pieces[0][0][:tiles]
    return [jnp.stack(parts) for parts in pieces], small, incoming


def spread_kernel(core_ref, sums_in_ref, sums_out_ref, *refs):
    w_in_ref, w_out_ref = refs[-2:]
    width, hidden = w_in_ref.shape[1:]
    per = width // 16
    for q in range(hidden // 128):
        at = slice(q * 128, (q + 1) * 128)
        w_in_ref[0, :, at] = sums_in_ref[0, q * per : (q + 1) * per].astype(F32).reshape(width, 128)
        out = sums_out_ref[0, q * per : (q + 1) * per].astype(F32).reshape(width, 128)
        w_out_ref[0, at, :] = jnp.transpose(out, (1, 0))


def place(core, width, hidden, sums_in, sums_out, before=()):
    half = sums_in.shape[0]
    shapes = ((EXPERTS, width, hidden), (EXPERTS, hidden, width))
    one = pl.BlockSpec((1,) + sums_in.shape[1:], lambda i, c: (i, 0, 0, 0))
    out_specs = tuple(pl.BlockSpec((1,) + s[1:], lambda i, c: (c[0] * half + i, 0, 0)) for s in shapes)
    return pl.pallas_call(
        spread_kernel,
        grid_spec=pltpu.PrefetchScalarGridSpec(
            num_scalar_prefetch=1,
            grid=(half,),
            in_specs=[one, one] + [pl.BlockSpec(memory_space=pl.ANY)] * len(before),
            out_specs=out_specs,
        ),
        out_shape=tuple(jax.ShapeDtypeStruct(s, F32) for s in shapes),
        input_output_aliases={3 + k: k for k in range(len(before))},
        compiler_params=params(32),
    )(core, sums_in, sums_out, *before)


def on_device(
    table,
    source_id,
    task_mask,
    feature_owner,
    feature_row,
    w_in,
    b_in,
    w_out,
    b_out,
    select_weight,
    mix_weight,
    cotangent,
):
    rows = source_id.shape[0]
    dp_count, outer_count = lax.axis_size("dp"), lax.axis_size("outer")
    devices = dp_count * outer_count
    index = lax.axis_index("dp") * outer_count + lax.axis_index("outer")
    vocab, width = table.shape
    per_row = feature_owner.shape[1]
    cap = 2 * per_row * rows // devices
    slots = devices * cap

    def exchange(x):
        return lax.all_to_all(x, AXES, split_axis=0, concat_axis=0, tiled=True)

    request, target, active = prepare(
        source_id.reshape(1, rows), task_mask.T, feature_owner.T, feature_row.T, devices, cap
    )
    arrived = exchange(request)
    weight_rows = (jnp.float32(rows * devices) / jnp.sum(arrived[:, cap]).astype(F32)).reshape(1)
    named = arrived[:, :cap].reshape(slots // 128, 128)
    found = find(named, table)
    replied = exchange(found.reshape(devices, cap, width)).reshape(slots, width)

    select = select_weight.T.reshape(NTASK, KSEL, BITS, width).transpose(2, 1, 0, 3)
    mix = mix_weight.T.reshape(NTASK, KSEL, width).transpose(1, 0, 2)
    gates = jnp.concatenate([select.reshape(BITS * KSEL, NTASK, width), mix])
    gates = jnp.concatenate([gates, gates], axis=1).reshape(-1, width)
    core = (index // outer_count) % 2
    keep_in, keep_out, send_in, send_out, outgoing, mixed, small = experts(
        weight_rows,
        core.reshape(1).astype(I32),
        active,
        target,
        replied,
        cotangent,
        w_in,
        b_in,
        w_out,
        b_out,
        gates,
    )

    incoming = exchange(outgoing.reshape(devices, cap, width)).reshape(slots, width)
    (mine_in, mine_out), small, incoming = sum_weights(
        (keep_in, keep_out), (send_in, send_out), small, incoming, index, dp_count, outer_count
    )
    table_sum = scatter(weight_rows, named, incoming, vocab)
    mine_in, mine_out, table_sum = tied(mine_in, mine_out, table_sum)
    core_here = core.reshape(1).astype(I32)
    hidden = w_in.shape[2]
    placed = place(core_here, width, hidden, mine_in, mine_out)
    others = [swap(m, outer_count, devices) for m in (mine_in, mine_out)]
    w_in_sum, w_out_sum = place(1 - core_here, width, hidden, *others, placed)
    small = small[:SMALL].reshape(4 * SMALL, 4, 128)

    def wide(x):
        return x.transpose(1, 0, 2).reshape(x.shape[1], -1)

    lanes = width // 128
    groups = small[: 12 * lanes].reshape(12, lanes, NTASK, 128).transpose(0, 2, 1, 3).reshape(12, NTASK, width)
    select_sum = groups[:8].reshape(BITS, KSEL, NTASK, width).transpose(2, 1, 0, 3).reshape(32, width).T
    mix_sum = groups[8:].reshape(KSEL, NTASK, width).transpose(1, 0, 2).reshape(16, width).T
    rest = small[12 * lanes :]
    chunks = hidden // 128
    b_out_sum = wide(rest[:lanes])
    b_in_sum = wide(rest[lanes : lanes + chunks])
    entropy_mean = jnp.sum(rest[lanes + chunks : lanes + chunks + rows // 128]) * weight_rows[0] / (rows * devices)
    return (
        mixed,
        table_sum,
        w_in_sum,
        b_in_sum,
        w_out_sum,
        b_out_sum,
        select_sum,
        mix_sum,
        entropy_mean,
    )


def solution(mesh):
    rows = P(AXES)
    flat = P(AXES, None)
    cube = P(AXES, None, None)
    placed = (flat, rows, P(), flat, flat, P(), P(), P(), P(), P(), P(), cube)
    return jax.shard_map(
        on_device,
        mesh=mesh,
        in_specs=placed,
        out_specs=(cube, flat, P(), P(), P(), P(), P(), P(), P()),
        check_vma=False,
    )
```

```python
import jax
import jax.numpy as jnp
from jax import lax
from jax.experimental import pallas as pl
from jax.experimental.pallas import tpu as pltpu
from jax.sharding import PartitionSpec as P

AXES = ("dp", "outer")
EXPERTS = 4
BITS = 2
KSEL = 4
NTASK = 4
ENTROPY_WEIGHT = 0.5
LOG_GUARD = 1e-06
SMOOTH_HALF = 5.0
SMALL = 11

F32, BF16, I32 = jnp.float32, jnp.bfloat16, jnp.int32
VMEM = pl.BlockSpec(memory_space=pltpu.VMEM)
HBM = pl.BlockSpec(memory_space=pl.ANY)
NT = (((1,), (1,)), ((), ()))
TN = (((0,), (0,)), ((), ()))
NN = (((1,), (0,)), ((), ()))


def dot(a, b, dims=NN):
    return lax.dot_general(a, b, dims, preferred_element_type=F32)


def iota(shape, axis):
    return lax.broadcasted_iota(I32, shape, axis)


def params(mib):
    return pltpu.CompilerParams(vmem_limit_bytes=mib << 20)


def index_kernel(*refs):
    given, (send_ref, target_ref, active_ref), held, sem = refs[:4], refs[4:7], refs[7:11], refs[11]
    copies = [pltpu.make_async_copy(g, h, sem.at[k]) for k, (g, h) in enumerate(zip(given, held))]
    for copy in copies:
        copy.start()
    for copy in copies:
        copy.wait()
    source_ref, mask_ref, owner_ref, row_ref = held
    owners, cap = send_ref.shape[0], send_ref.shape[2] // 2
    rows = owner_ref.shape[1]
    step = 256
    before = (iota((step, step), 0) < iota((step, step), 1)).astype(BF16)
    carry = jnp.zeros((owners, 1), F32)
    high = jnp.zeros((owners, cap), F32)
    low = jnp.zeros((owners, cap), F32)
    for f in range(owner_ref.shape[0]):
        for start in range(0, rows, step):
            owner = owner_ref[f : f + 1, start : start + step]
            row = row_ref[f : f + 1, start : start + step]
            named = (owner == iota((owners, step), 0)).astype(F32)
            named_low = named.astype(BF16)
            earlier = dot(named_low, before) + carry
            carry = carry + jnp.sum(named, axis=1, keepdims=True)
            slot = jnp.sum(named * earlier, axis=0, keepdims=True).astype(I32)
            target_ref[f : f + 1, start : start + step] = owner * cap + slot
            at_slot = (slot == iota((cap, step), 0)).astype(F32).astype(BF16)
            high = high + dot((named * (row >> 8).astype(F32)).astype(BF16), at_slot, NT)
            low = low + dot((named * (row & 255).astype(F32)).astype(BF16), at_slot, NT)
    send_ref[:, 0, :cap] = (high * 256.0 + low).astype(I32)
    sources = mask_ref.shape[1]
    from_source = (source_ref[...] == iota((sources, rows), 0)).astype(F32).astype(BF16)
    active = dot(mask_ref[...].astype(F32).astype(BF16), from_source)
    active_ref[...] = active
    count = jnp.sum(jnp.sum(active, axis=0, keepdims=True), axis=1, keepdims=True)
    send_ref[:, 0, cap:] = jnp.broadcast_to(count, (owners, cap)).astype(I32)


def prepare(source, mask_t, owner_t, row_t, owners, cap):
    rows = owner_t.shape[1]
    return pl.pallas_call(
        index_kernel,
        out_shape=(
            jax.ShapeDtypeStruct((owners, 1, 2 * cap), I32),
            jax.ShapeDtypeStruct(owner_t.shape, I32),
            jax.ShapeDtypeStruct((mask_t.shape[0], rows), F32),
        ),
        in_specs=[HBM] * 4,
        out_specs=(VMEM,) * 3,
        scratch_shapes=[pltpu.VMEM(x.shape, I32) for x in (source, mask_t, owner_t, row_t)]
        + [pltpu.SemaphoreType.DMA((4,))],
        compiler_params=params(60),
    )(source, mask_t, owner_t, row_t)


def find_kernel(named_ref, table_ref, found_ref):
    slots = found_ref.shape[0]
    per = slots // 128
    first = pl.program_id(0) * per
    blocks = table_ref.shape[0] // 128
    columns = jnp.transpose(named_ref[pl.ds(pl.multiple_of(first, per), per), :128].astype(F32), (1, 0))
    parts = []
    for line in range(per):
        column = jnp.broadcast_to(columns[:, line : line + 1], (128, 128)).astype(I32)
        high = (column >> 7).astype(F32).astype(BF16)
        low = ((column & 127) == iota((128, 128), 1)).astype(F32).astype(BF16)
        parts.append((high, low))
    high = jnp.concatenate([p[0] for p in parts], axis=0)
    low = jnp.concatenate([p[1] for p in parts], axis=0)
    zero = jnp.zeros_like(low)
    picks = jnp.concatenate([jnp.where(high == jnp.bfloat16(b), low, zero) for b in range(blocks)], axis=1)
    found_ref[...] = dot(picks, table_ref[...]).astype(BF16)


def find(named, table):
    lines = named.shape[0]
    slots = lines * 128
    step = 1024
    return pl.pallas_call(
        find_kernel,
        grid=(slots // step,),
        out_shape=jax.ShapeDtypeStruct((slots, table.shape[1]), BF16),
        in_specs=[
            pl.BlockSpec(named.shape, lambda i: (0, 0)),
            pl.BlockSpec(table.shape, lambda i: (0, 0)),
        ],
        out_specs=pl.BlockSpec((step, table.shape[1]), lambda i: (i, 0)),
        compiler_params=params(60),
    )(named, table)


def scatter_kernel(scale_ref, named_ref, incoming_ref, sum_ref, pick_ref):
    count = sum_ref.shape[0] // 128
    base = pl.program_id(0) * count
    pieces = 4
    lines = named_ref.shape[0] // pieces
    zero, one = jnp.bfloat16(0), jnp.bfloat16(1)

    def build(q):
        for line in range(q * lines, (q + 1) * lines):
            row = named_ref[line : line + 1, :128]
            high = jnp.broadcast_to(row >> 7, (16, 128)).astype(F32).astype(BF16)
            low = ((row & 127) == iota((128, 128), 0)).astype(F32).astype(BF16).reshape(8, 16, 128)
            for b in range(count):
                here = jnp.where(high == (base + b).astype(F32).astype(BF16), one, zero)[None]
                pick_ref[b * 128 : (b + 1) * 128, line * 128 : (line + 1) * 128] = (low * here).reshape(128, 128)

    build(0)
    total = jnp.zeros(sum_ref.shape, F32)
    for q in range(pieces):
        if q + 1 < pieces:
            build(q + 1)
        at = slice(q * lines * 128, (q + 1) * lines * 128)
        total = total + dot(pick_ref[:, at], incoming_ref[at, :])
    sum_ref[...] = total * scale_ref[0]


def scatter(scale, named, incoming, vocab):
    step = 1024
    width = incoming.shape[1]
    return pl.pallas_call(
        scatter_kernel,
        grid=(vocab // step,),
        out_shape=jax.ShapeDtypeStruct((vocab, width), F32),
        in_specs=[
            pl.BlockSpec(memory_space=pltpu.SMEM),
            pl.BlockSpec(named.shape, lambda i: (0, 0)),
            pl.BlockSpec(incoming.shape, lambda i: (0, 0)),
        ],
        out_specs=pl.BlockSpec((step, width), lambda i: (i, 0)),
        scratch_shapes=[pltpu.VMEM((step, named.shape[0] * 128), BF16)],
        compiler_params=params(48),
    )(scale, named, incoming)


def smooth(v):
    c = jnp.clip(v, -SMOOTH_HALF, SMOOTH_HALF)
    return -0.002 * c * c * c + 0.15 * c + 0.5


def smooth_slope(v):
    c = jnp.clip(v, -SMOOTH_HALF, SMOOTH_HALF)
    inside = jnp.where((v >= -SMOOTH_HALF) & (v <= SMOOTH_HALF), 1.0, 0.0)
    return inside * (0.15 - 0.006 * c * c)


def main_kernel(
    scale_ref,
    core_ref,
    active_ref,
    b_in_ref,
    b_out_ref,
    gates_ref,
    target_ref,
    replied_ref,
    cot_hbm,
    w_in_hbm,
    w_out_hbm,
    keep_in_hbm,
    keep_out_hbm,
    send_in_hbm,
    send_out_hbm,
    outgoing_hbm,
    mixed_hbm,
    small_ref,
    outgoing_ref,
    mixed_ref,
    fill_ref,
    pick_ref,
    cot_ref,
    w_in_ref,
    w_out_ref,
    result_ref,
    hidden_ref,
    hidden_up_ref,
    w_in_low,
    w_out_low,
    b_in_sum,
    b_out_sum,
    in_sem,
    out_sem,
):
    rows = active_ref.shape[1]
    part = 64
    blocks = rows // part
    flat = part * NTASK
    slots, width = replied_ref.shape
    hidden_width = w_in_ref.shape[2]
    chunk = 256
    chunks = hidden_width // chunk
    half = EXPERTS // 2
    zero16 = jnp.bfloat16(0)

    loads = {}

    def load(name, source, target):
        loads[name] = pltpu.make_async_copy(source, target, in_sem.at[len(loads)])
        loads[name].start()

    def loaded(name):
        if name in loads:
            loads.pop(name).wait()

    load(("in", 0), w_in_hbm.at[0], w_in_ref.at[0])
    load("cot", cot_hbm, cot_ref)
    load(("out", 0), w_out_hbm.at[0], w_out_ref.at[0])
    for e in range(1, EXPERTS):
        load(("in", e), w_in_hbm.at[e], w_in_ref.at[e])
        load(("out", e), w_out_hbm.at[e], w_out_ref.at[e])

    stores = []

    def store(source, target):
        stores.append(pltpu.make_async_copy(source, target, out_sem.at[len(stores)]))
        stores[-1].start()

    target = target_ref[...]
    columns = jnp.transpose(jnp.concatenate([target >> 7, target & 127] * 2, axis=0).astype(F32), (1, 0))

    def spread(k):
        return jnp.broadcast_to(columns[:, k : k + 1], (rows, 128))

    highs = [spread(f).astype(BF16) for f in range(2)]
    lows = [(spread(2 + f).astype(I32) == iota((rows, 128), 1)).astype(F32).astype(BF16) for f in range(2)]
    pieces = 4
    lines = slots // 128 // pieces

    def pick(p):
        for b in range(p * lines, (p + 1) * lines):
            first = jnp.where(highs[0] == jnp.bfloat16(b), lows[0], zero16)
            pick_ref[:, b * 128 : (b + 1) * 128] = jnp.where(highs[1] == jnp.bfloat16(b), lows[1], first)

    inputs = jnp.zeros((rows, width), F32)
    wide_rows = rows // 128
    at_high, at_low = [], []
    for piece in range(wide_rows):
        at = target[:, piece * 128 : (piece + 1) * 128]
        at_high.append([jnp.broadcast_to(at[f : f + 1, :] >> 7, (16, 128)).astype(F32).astype(BF16) for f in range(2)])
        low = [(at[f : f + 1, :] & 127) == iota((128, 128), 0) for f in range(2)]
        at_low.append([x.astype(F32).astype(BF16).reshape(8, 16, 128) for x in low])

    def fill(line):
        for piece in range(wide_rows):
            here = [jnp.where(h == jnp.bfloat16(line), jnp.bfloat16(1), zero16)[None] for h in at_high[piece]]
            fill_ref[line * 128 : (line + 1) * 128, piece * 128 : (piece + 1) * 128] = (
                at_low[piece][0] * here[0] + at_low[piece][1] * here[1]
            ).reshape(128, 128)

    for line in range(slots // 128):
        fill(line)
    inputs_t = dot(replied_ref[...], fill_ref[...], TN).astype(BF16)
    inputs = jnp.transpose(inputs_t, (1, 0))

    gates_w = gates_ref[...]
    once = jnp.where((iota(gates_w.shape, 0) & 4) == 0, gates_w, zero16)
    logits = dot(gates_w, inputs, NT)
    active = active_ref[...]
    active = jnp.concatenate([active, active], axis=0)
    along = iota((part, flat), 0) == (iota((part, flat), 1) >> 2)
    repeat = along.astype(F32).astype(BF16)
    own_task = iota((8, flat), 0) == (iota((8, flat), 1) & 3)

    def group(k):
        return logits[8 * k : 8 * k + 8, :]

    zetas = [[group(n * KSEL + c) for c in range(KSEL)] for n in range(BITS)]
    levels = [[smooth(z) for z in zs] for zs in zetas]
    mix = [group(BITS * KSEL + c) for c in range(KSEL)]
    top = jnp.maximum(jnp.maximum(mix[0], mix[1]), jnp.maximum(mix[2], mix[3]))
    mix = [jnp.exp(m - top) for m in mix]
    total = 1.0 / (mix[0] + mix[1] + mix[2] + mix[3])
    mix = [m * total for m in mix]
    chosen = [
        [
            (levels[0][c] if e & 1 else 1.0 - levels[0][c]) * (levels[1][c] if e & 2 else 1.0 - levels[1][c])
            for e in range(EXPERTS)
        ]
        for c in range(KSEL)
    ]
    gate = [sum(mix[c] * chosen[c][e] for c in range(KSEL)) * active for e in range(EXPERTS)]

    loaded("cot")
    ups, gate_rows = [], []
    for b in range(blocks):
        g = [x[:, b * part : (b + 1) * part] for x in gate]
        gate_rows.append(jnp.concatenate(g, axis=1).astype(BF16))
        wide = dot(jnp.concatenate(g, axis=0).astype(BF16), repeat)
        mats = []
        for e in range(EXPERTS):
            row = jnp.sum(jnp.where(own_task, wide[8 * e : 8 * e + 8, :], 0.0), axis=0, keepdims=True)
            row = jnp.broadcast_to(row, (part, flat)).astype(BF16)
            mats.append(jnp.where(along, row, zero16))
        cot = cot_ref[b * part : (b + 1) * part].reshape(flat, width)
        ups.append(dot(jnp.concatenate(mats, axis=0), cot))
    result_up = [jnp.concatenate([u[e * part : (e + 1) * part, :] for u in ups], axis=0) for e in range(EXPERTS)]
    result_low = [u.astype(BF16) for u in result_up]

    def into_tiles(low, e, part):
        part = part * scale_ref[0]
        per = width // 16
        for q in range(hidden_width // 128):
            low[e, q * per : (q + 1) * per] = part[:, q * 128 : (q + 1) * 128].astype(BF16).reshape(per, 16, 128)

    def first_layer(e, c):
        loaded(("in", e))
        loaded(("out", e))
        at = slice(c * chunk, (c + 1) * chunk)
        pre = dot(inputs, w_in_ref[e, :, at]) + b_in_ref[e : e + 1, at].astype(F32)
        logistic = 0.5 * jnp.tanh(0.5 * pre) + 0.5
        hidden = pre * logistic
        slope = logistic + hidden - hidden * logistic
        hidden_ref[e % 2, :, at] = hidden.astype(BF16)
        hidden_up = dot(result_low[e], w_out_ref[e, at, :], NT) * slope
        b_in_sum[e : e + 1, at] = jnp.sum(hidden_up, axis=0, keepdims=True)
        hidden_up_ref[e % 2, :, at] = hidden_up.astype(BF16)

    input_up = jnp.zeros((rows, width), F32)

    def second_layer(e, c):
        nonlocal input_up
        if c == 0:
            result = dot(hidden_ref[e % 2], w_out_ref[e]) + b_out_ref[e : e + 1, :].astype(F32)
            result = result.astype(BF16)
            result_ref[:, e] = result.reshape(blocks, part, width)
            b_out_sum[e : e + 1, :] = jnp.sum(result_up[e], axis=0, keepdims=True)
        elif c == 1:
            input_up = input_up + dot(hidden_up_ref[e % 2], w_in_ref[e], NT)
        elif c == 2:
            into_tiles(w_in_low, e, dot(inputs_t, hidden_up_ref[e % 2]))
        else:
            into_tiles(w_out_low, e, dot(jnp.transpose(result_low[e], (1, 0)), hidden_ref[e % 2]))

    for c in range(chunks):
        first_layer(0, c)
    for e in range(EXPERTS):
        for c in range(chunks):
            if e + 1 < EXPERTS:
                first_layer(e + 1, c)
            second_layer(e, c)

    core = core_ref[0]
    for i in range(half):
        mine = core * half + i
        other = (1 - core) * half + i
        store(w_in_low.at[mine], keep_in_hbm.at[i])
        store(w_out_low.at[mine], keep_out_hbm.at[i])
        store(w_in_low.at[other], send_in_hbm.at[i])
        store(w_out_low.at[other], send_out_hbm.at[i])

    down = (iota((flat, flat), 0) >> 2) == (iota((flat, flat), 1) & (part - 1))
    gate_up = [[] for _ in range(EXPERTS)]
    for b in range(blocks):
        cot = cot_ref[b * part : (b + 1) * part].reshape(flat, width)
        products = jnp.where(down, dot(cot, result_ref[b].reshape(flat, width), NT), 0.0)
        p = jnp.sum(products.reshape(flat // 8, 8, flat), axis=0)
        p = p + jnp.concatenate([p[4:], p[:4]], axis=0)
        for e in range(EXPERTS):
            gate_up[e].append(p[:, e * part : (e + 1) * part])
    gate_up = [jnp.concatenate(g, axis=1) * active for g in gate_up]
    level_up = [[None] * KSEL for _ in range(BITS)]
    mixing_up = []
    entropy = 0.0
    for c in range(KSEL):
        mixing_up.append(sum(gate_up[e] * chosen[c][e] for e in range(EXPERTS)))
        chosen_up = []
        for e in range(EXPERTS):
            x = chosen[c][e]
            log = jnp.log(x + LOG_GUARD)
            entropy = entropy - x * log
            chosen_up.append(gate_up[e] * mix[c] - (ENTROPY_WEIGHT * active) * (log + x / (x + LOG_GUARD)))
        l0, l1 = levels[0][c], levels[1][c]
        level_up[0][c] = (chosen_up[1] - chosen_up[0]) * (1.0 - l1) + (chosen_up[3] - chosen_up[2]) * l1
        level_up[1][c] = (chosen_up[2] - chosen_up[0]) * (1.0 - l0) + (chosen_up[3] - chosen_up[1]) * l0
    entropy = (active * entropy)[:4, :]
    mean_up = sum(mixing_up[c] * mix[c] for c in range(KSEL))
    ups_all = [level_up[n][c] * smooth_slope(zetas[n][c]) for n in range(BITS) for c in range(KSEL)]
    ups_all += [mix[c] * (mixing_up[c] - mean_up) for c in range(KSEL)]
    logits_up = jnp.concatenate(ups_all, axis=0)
    up_high = logits_up.astype(BF16)
    up_low = (logits_up - up_high.astype(F32)).astype(BF16)
    input_up = (input_up + dot(up_high, once, TN) + dot(up_low, once, TN)).astype(BF16)
    for b in range(blocks):
        mats = jnp.where(down, jnp.concatenate([gate_rows[b]] * (flat // 8), axis=0), zero16)
        mixed = dot(mats, result_ref[b].reshape(flat, width))
        mixed_ref[b * part : (b + 1) * part] = mixed.reshape(part, NTASK, width).astype(BF16)
    store(mixed_ref, mixed_hbm)
    span = slots // pieces
    for p in range(pieces):
        at = pl.ds(p * span, span)
        outgoing_ref[at, :] = dot(fill_ref[at, :], input_up).astype(BF16)
        store(outgoing_ref.at[at], outgoing_hbm.at[at])

    scale = scale_ref[0]
    gates_sum = (dot(up_high, inputs) + dot(up_low, inputs)) * scale
    small_ref[...] = jnp.zeros_like(small_ref)
    n = 0

    def put(values):
        nonlocal n
        for q in range(values.shape[1] // 128):
            small_ref[n // 4, n % 4 * 4 : n % 4 * 4 + 4, :] = values[:, q * 128 : (q + 1) * 128]
            n += 1

    for k in range(12):
        put(gates_sum[8 * k : 8 * k + 4, :])
    put(b_out_sum[...] * scale)
    put(b_in_sum[...] * scale)
    put(entropy)
    for copy in stores:
        copy.wait()


def experts(scale, core, active, target, replied, cot, w_in, b_in, w_out, b_out, gates):
    rows, slots = active.shape[1], replied.shape[0]
    width, hidden = w_in.shape[1], w_in.shape[2]
    smem = pl.BlockSpec(memory_space=pltpu.SMEM)
    hbm = pl.BlockSpec(memory_space=pl.ANY)
    grads = jax.ShapeDtypeStruct((EXPERTS // 2, width * hidden // 2048, 16, 128), BF16)
    low = pltpu.VMEM((EXPERTS,) + grads.shape[1:], BF16)
    act = pltpu.VMEM((2, rows, hidden), BF16)
    result = (rows // 64, EXPERTS, 64, width)
    near = pltpu.with_memory_space_constraint(replied, pltpu.VMEM)
    return pl.pallas_call(
        main_kernel,
        out_shape=(
            grads,
            grads,
            grads,
            grads,
            jax.ShapeDtypeStruct((slots, width), BF16),
            jax.ShapeDtypeStruct(cot.shape, BF16),
            jax.ShapeDtypeStruct((SMALL, 16, 128), F32),
        ),
        in_specs=[smem, smem] + [VMEM] * 6 + [hbm] * 3,
        out_specs=(hbm,) * 6 + (VMEM,),
        scratch_shapes=[
            pltpu.VMEM((slots, width), BF16),
            pltpu.VMEM(cot.shape, BF16),
            pltpu.VMEM((slots, rows), BF16),
            pltpu.VMEM((rows, slots), BF16),
            pltpu.VMEM(cot.shape, BF16),
            pltpu.VMEM(w_in.shape, BF16),
            pltpu.VMEM(w_out.shape, BF16),
            pltpu.VMEM(result, BF16),
            act,
            act,
            low,
            low,
            pltpu.VMEM((EXPERTS, hidden), F32),
            pltpu.VMEM((EXPERTS, width), F32),
            pltpu.SemaphoreType.DMA((1 + 2 * EXPERTS,)),
            pltpu.SemaphoreType.DMA((4 * EXPERTS // 2 + 5,)),
        ],
        compiler_params=params(56),
    )(scale, core, active, b_in, b_out, gates, target, near, cot, w_in, w_out)


def swap(x, mask, devices):
    return lax.ppermute(x, AXES, [(i, i ^ mask) for i in range(devices)])


def bits_of(count):
    return range(count.bit_length() - 1)


def sum_over_devices(x, devices):
    for k in bits_of(devices):
        x = x + swap(x, 1 << k, devices)
    return x


def halves(x, bit):
    rows = x.shape[0] // 2
    keep = lax.dynamic_slice_in_dim(x, bit * rows, rows, 0)
    give = lax.dynamic_slice_in_dim(x, (1 - bit) * rows, rows, 0)
    return keep, give.astype(BF16)


def joined(mine, other, bit):
    return jnp.where(bit == 0, jnp.concatenate([mine, other]), jnp.concatenate([other, mine]))


def tied(*values):
    return lax.optimization_barrier(values)


def sum_weights(keeps, sends, small, incoming, index, dp_count, outer_count):
    devices = dp_count * outer_count
    core = outer_count
    outer = [1 << k for k in bits_of(outer_count)]
    across = [outer_count << k for k in bits_of(dp_count)][1:]
    first = [outer[0], across[0]]
    rest = outer[1:] + across[1:]

    def bit(mask):
        return (index // mask) % 2

    share = -(-small.shape[0] // devices) * devices // 2
    small = jnp.pad(small, ((0, 2 * share - small.shape[0]), (0, 0), (0, 0)))
    mine, others = halves(small, bit(core))
    tiles = keeps[0].shape[1]
    got = [swap(send, core, devices) for send in sends] + [swap(others, core, devices)]
    pieces = [[k for k in keep.astype(F32) + g.astype(F32)] for keep, g in zip(keeps, got)]
    pieces[0][0] = jnp.concatenate([pieces[0][0], mine + got[-1].astype(F32)])
    for orders in (first, first[::-1]):
        for n, parts in enumerate(pieces):
            split = [halves(p, bit(m)) for p, m in zip(parts, orders)]
            pieces[n] = [k + swap(g, m, devices).astype(F32) for (k, g), m in zip(split, orders)]
    for mask in rest:
        for n, parts in enumerate(pieces):
            split = [halves(p, bit(mask)) for p in parts]
            cut = split[0][0].shape[0]
            got = swap(jnp.concatenate([g for _, g in split]), mask, devices).astype(F32)
            pieces[n] = [split[0][0] + got[:cut], split[1][0] + got[cut:]]
    pieces = [[p.astype(BF16) for p in parts] for parts in pieces]
    for mask in rest[::-1]:
        for n, parts in enumerate(pieces):
            cut = parts[0].shape[0]
            got = swap(jnp.concatenate(parts), mask, devices)
            pieces[n] = [joined(parts[0], got[:cut], bit(mask)), joined(parts[1], got[cut:], bit(mask))]
    for step, orders in enumerate((first[::-1], first)):
        pieces = [[joined(p, swap(p, m, devices), bit(m)) for p, m in zip(parts, orders)] for parts in pieces]
        if step == 0:
            pieces, incoming = tied(pieces, incoming)
    small = pieces[0][0][tiles:]
    small = (small, swap(small, core, devices))
    pieces[0][0] = pieces[0][0][:tiles]
    return [jnp.stack(parts) for parts in pieces], small, incoming


def spread(sums_in_ref, sums_out_ref, w_in_ref, w_out_ref):
    width, hidden = w_in_ref.shape[1:]
    per = width // 16
    for q in range(hidden // 128):
        at = slice(q * 128, (q + 1) * 128)
        w_in_ref[0, :, at] = sums_in_ref[0, q * per : (q + 1) * per].astype(F32).reshape(width, 128)
        out = sums_out_ref[0, q * per : (q + 1) * per].astype(F32).reshape(width, 128)
        w_out_ref[0, at, :] = jnp.transpose(out, (1, 0))


def place_kernel(core_ref, sums_in_ref, sums_out_ref, w_in_ref, w_out_ref):
    spread(sums_in_ref, sums_out_ref, w_in_ref, w_out_ref)


def last_kernel(
    core_ref,
    sums_in_ref,
    sums_out_ref,
    mine_ref,
    other_ref,
    scale_ref,
    _,
    __,
    w_in_ref,
    w_out_ref,
    select_ref,
    mix_ref,
    b_in_ref,
    b_out_ref,
    entropy_ref,
    small_ref,
):
    spread(sums_in_ref, sums_out_ref, w_in_ref, w_out_ref)

    @pl.when(pl.program_id(0) == 0)
    def _():
        share = mine_ref.shape[0]
        small_ref[pl.ds((1 - core_ref[0]) * share, share)] = mine_ref[...].astype(F32)
        small_ref[pl.ds(core_ref[0] * share, share)] = other_ref[...].astype(F32)
        n = 0

        def take(blocks):
            nonlocal n
            got = [small_ref[(n + q) // 4, (n + q) % 4 * 4 : (n + q) % 4 * 4 + 4, :] for q in range(blocks)]
            n += blocks
            return got

        width = b_out_ref.shape[1]
        lanes = width // 128
        for k in range(BITS * KSEL + KSEL):
            got = jnp.concatenate(take(lanes), axis=1)
            for t in range(NTASK):
                if k < BITS * KSEL:
                    row = t * KSEL * BITS + k % KSEL * BITS + k // KSEL
                    select_ref[row : row + 1, :] = got[t : t + 1, :]
                else:
                    row = t * KSEL + k % KSEL
                    mix_ref[row : row + 1, :] = got[t : t + 1, :]
        b_out_ref[...] = jnp.concatenate(take(lanes), axis=1)
        b_in_ref[...] = jnp.concatenate(take(b_in_ref.shape[1] // 128), axis=1)
        total = jnp.sum(sum(take(4 * SMALL - n)), axis=0, keepdims=True)
        entropy_ref[...] = jnp.sum(total, axis=1, keepdims=True) * scale_ref[0]


def place(core, width, hidden, sums_in, sums_out, before=(), small=()):
    half = sums_in.shape[0]
    shapes = ((EXPERTS, width, hidden), (EXPERTS, hidden, width))
    one = pl.BlockSpec((1,) + sums_in.shape[1:], lambda i, c: (i, 0, 0, 0))
    out_specs = tuple(pl.BlockSpec((1,) + s[1:], lambda i, c: (c[0] * half + i, 0, 0)) for s in shapes)
    in_specs = [one, one]
    scratch = []
    if small:
        rest = ((NTASK * KSEL * BITS, width), (NTASK * KSEL, width), (EXPERTS, hidden), (EXPERTS, width), (1, 1))
        shapes += rest
        out_specs += tuple(pl.BlockSpec(s, lambda i, c: (0, 0)) for s in rest)
        in_specs += [pl.BlockSpec(x.shape, lambda i, c: (0, 0, 0)) for x in small[:2]]
        in_specs.append(pl.BlockSpec(memory_space=pltpu.SMEM))
        scratch = [pltpu.VMEM((2 * small[0].shape[0],) + small[0].shape[1:], F32)]
    return pl.pallas_call(
        last_kernel if small else place_kernel,
        grid_spec=pltpu.PrefetchScalarGridSpec(
            num_scalar_prefetch=1,
            grid=(half,),
            in_specs=in_specs + [HBM] * len(before),
            out_specs=out_specs,
            scratch_shapes=scratch,
        ),
        out_shape=tuple(jax.ShapeDtypeStruct(s, F32) for s in shapes),
        input_output_aliases={1 + len(in_specs) + k: k for k in range(len(before))},
        compiler_params=params(32),
    )(core, sums_in, sums_out, *small, *before)


def on_device(
    table,
    source_id,
    task_mask,
    feature_owner,
    feature_row,
    w_in,
    b_in,
    w_out,
    b_out,
    select_weight,
    mix_weight,
    cotangent,
):
    rows = source_id.shape[0]
    dp_count, outer_count = lax.axis_size("dp"), lax.axis_size("outer")
    devices = dp_count * outer_count
    index = lax.axis_index("dp") * outer_count + lax.axis_index("outer")
    vocab, width = table.shape
    per_row = feature_owner.shape[1]
    cap = 2 * per_row * rows // devices
    slots = devices * cap

    def exchange(x):
        return lax.all_to_all(x, AXES, split_axis=0, concat_axis=0, tiled=True)

    request, target, active = prepare(
        source_id.reshape(1, rows), task_mask.T, feature_owner.T, feature_row.T, devices, cap
    )
    arrived = exchange(request).reshape(devices, 2 * cap)
    weight_rows = (jnp.float32(rows * devices) / jnp.sum(arrived[:, cap]).astype(F32)).reshape(1)
    named = arrived if cap == 128 else arrived[:, :cap].reshape(slots // 128, 128)
    found = find(named, table)
    replied = exchange(found.reshape(devices, cap, width)).reshape(slots, width)

    select = select_weight.T.reshape(NTASK, KSEL, BITS, width).transpose(2, 1, 0, 3)
    mix = mix_weight.T.reshape(NTASK, KSEL, width).transpose(1, 0, 2)
    gates = jnp.concatenate([select.reshape(BITS * KSEL, NTASK, width), mix])
    gates = jnp.concatenate([gates, gates], axis=1).reshape(-1, width)
    core = (index // outer_count) % 2
    keep_in, keep_out, send_in, send_out, outgoing, mixed, small = experts(
        weight_rows,
        core.reshape(1).astype(I32),
        active,
        target,
        replied,
        cotangent,
        w_in,
        b_in,
        w_out,
        b_out,
        gates,
    )

    incoming = exchange(outgoing.reshape(devices, cap, width)).reshape(slots, width)
    (mine_in, mine_out), small, incoming = sum_weights(
        (keep_in, keep_out), (send_in, send_out), small, incoming, index, dp_count, outer_count
    )
    table_sum = scatter(weight_rows, named, incoming, vocab)
    mine_in, mine_out, table_sum = tied(mine_in, mine_out, table_sum)
    core_here = core.reshape(1).astype(I32)
    hidden = w_in.shape[2]
    placed = place(core_here, width, hidden, mine_in, mine_out)
    others = [swap(m, outer_count, devices) for m in (mine_in, mine_out)]
    w_in_sum, w_out_sum, select_sum, mix_sum, b_in_sum, b_out_sum, entropy = place(
        1 - core_here, width, hidden, *others, placed, small + (weight_rows / (rows * devices),)
    )
    return (
        mixed,
        table_sum,
        w_in_sum,
        b_in_sum,
        w_out_sum,
        b_out_sum,
        select_sum.T,
        mix_sum.T,
        entropy.reshape(()),
    )


def solution(mesh):
    rows = P(AXES)
    flat = P(AXES, None)
    cube = P(AXES, None, None)
    placed = (flat, rows, P(), flat, flat, P(), P(), P(), P(), P(), P(), cube)
    return jax.shard_map(
        on_device,
        mesh=mesh,
        in_specs=placed,
        out_specs=(cube, flat, P(), P(), P(), P(), P(), P(), P()),
        check_vma=False,
    )
```

```python
import jax
import jax.numpy as jnp
from jax import lax
from jax.experimental import pallas as pl
from jax.experimental.pallas import tpu as pltpu
from jax.sharding import PartitionSpec as P

AXES = ("dp", "outer")
EXPERTS = 4
BITS = 2
KSEL = 4
NTASK = 4
ENTROPY_WEIGHT = 0.5
LOG_GUARD = 1e-06
SMOOTH_HALF = 5.0
SMALL = 11

F32, BF16, I32 = jnp.float32, jnp.bfloat16, jnp.int32
VMEM = pl.BlockSpec(memory_space=pltpu.VMEM)
HBM = pl.BlockSpec(memory_space=pl.ANY)
NT = (((1,), (1,)), ((), ()))
TN = (((0,), (0,)), ((), ()))
NN = (((1,), (0,)), ((), ()))


def dot(a, b, dims=NN):
    return lax.dot_general(a, b, dims, preferred_element_type=F32)


def iota(shape, axis):
    return lax.broadcasted_iota(I32, shape, axis)


def params(mib):
    return pltpu.CompilerParams(vmem_limit_bytes=mib << 20)


def index_kernel(*refs):
    given, (send_ref, target_ref, active_ref), held, sem = refs[:4], refs[4:7], refs[7:11], refs[11]
    copies = [pltpu.make_async_copy(g, h, sem.at[k]) for k, (g, h) in enumerate(zip(given, held))]
    for copy in copies:
        copy.start()
    for copy in copies:
        copy.wait()
    source_ref, mask_ref, owner_ref, row_ref = held
    owners, cap = send_ref.shape[0], send_ref.shape[2] // 2
    rows = owner_ref.shape[1]
    step = 256
    before = (iota((step, step), 0) < iota((step, step), 1)).astype(BF16)
    carry = jnp.zeros((owners, 1), F32)
    high = jnp.zeros((owners, cap), F32)
    low = jnp.zeros((owners, cap), F32)
    for f in range(owner_ref.shape[0]):
        for start in range(0, rows, step):
            owner = owner_ref[f : f + 1, start : start + step]
            row = row_ref[f : f + 1, start : start + step]
            named = (owner == iota((owners, step), 0)).astype(F32)
            named_low = named.astype(BF16)
            earlier = dot(named_low, before) + carry
            carry = carry + jnp.sum(named, axis=1, keepdims=True)
            slot = jnp.sum(named * earlier, axis=0, keepdims=True).astype(I32)
            target_ref[f : f + 1, start : start + step] = owner * cap + slot
            at_slot = (slot == iota((cap, step), 0)).astype(F32).astype(BF16)
            high = high + dot((named * (row >> 8).astype(F32)).astype(BF16), at_slot, NT)
            low = low + dot((named * (row & 255).astype(F32)).astype(BF16), at_slot, NT)
    send_ref[:, 0, :cap] = (high * 256.0 + low).astype(I32)
    sources = mask_ref.shape[1]
    from_source = (source_ref[...] == iota((sources, rows), 0)).astype(F32).astype(BF16)
    active = dot(mask_ref[...].astype(F32).astype(BF16), from_source)
    active_ref[...] = active
    count = jnp.sum(jnp.sum(active, axis=0, keepdims=True), axis=1, keepdims=True)
    send_ref[:, 0, cap:] = jnp.broadcast_to(count, (owners, cap)).astype(I32)


def prepare(source, mask_t, owner_t, row_t, owners, cap):
    rows = owner_t.shape[1]
    return pl.pallas_call(
        index_kernel,
        out_shape=(
            jax.ShapeDtypeStruct((owners, 1, 2 * cap), I32),
            jax.ShapeDtypeStruct(owner_t.shape, I32),
            jax.ShapeDtypeStruct((mask_t.shape[0], rows), F32),
        ),
        in_specs=[HBM] * 4,
        out_specs=(VMEM,) * 3,
        scratch_shapes=[pltpu.VMEM(x.shape, I32) for x in (source, mask_t, owner_t, row_t)]
        + [pltpu.SemaphoreType.DMA((4,))],
        compiler_params=params(60),
    )(source, mask_t, owner_t, row_t)


def find_kernel(named_ref, table_ref, found_ref):
    slots = found_ref.shape[0]
    per = slots // 128
    first = pl.program_id(0) * per
    blocks = table_ref.shape[0] // 128
    columns = jnp.transpose(named_ref[pl.ds(pl.multiple_of(first, per), per), :128].astype(F32), (1, 0))
    parts = []
    for line in range(per):
        column = jnp.broadcast_to(columns[:, line : line + 1], (128, 128)).astype(I32)
        high = (column >> 7).astype(F32).astype(BF16)
        low = ((column & 127) == iota((128, 128), 1)).astype(F32).astype(BF16)
        parts.append((high, low))
    high = jnp.concatenate([p[0] for p in parts], axis=0)
    low = jnp.concatenate([p[1] for p in parts], axis=0)
    zero = jnp.zeros_like(low)
    picks = jnp.concatenate([jnp.where(high == jnp.bfloat16(b), low, zero) for b in range(blocks)], axis=1)
    found_ref[...] = dot(picks, table_ref[...]).astype(BF16)


def find(named, table):
    lines = named.shape[0]
    slots = lines * 128
    step = 1024
    return pl.pallas_call(
        find_kernel,
        grid=(slots // step,),
        out_shape=jax.ShapeDtypeStruct((slots, table.shape[1]), BF16),
        in_specs=[
            pl.BlockSpec(named.shape, lambda i: (0, 0)),
            pl.BlockSpec(table.shape, lambda i: (0, 0)),
        ],
        out_specs=pl.BlockSpec((step, table.shape[1]), lambda i: (i, 0)),
        compiler_params=params(60),
    )(named, table)


def scatter_kernel(scale_ref, named_ref, incoming_ref, sum_ref, pick_ref):
    count = sum_ref.shape[0] // 128
    base = pl.program_id(0) * count
    pieces = 4
    lines = named_ref.shape[0] // pieces
    zero, one = jnp.bfloat16(0), jnp.bfloat16(1)

    def build(q):
        for line in range(q * lines, (q + 1) * lines):
            row = named_ref[line : line + 1, :128]
            high = jnp.broadcast_to(row >> 7, (16, 128)).astype(F32).astype(BF16)
            low = ((row & 127) == iota((128, 128), 0)).astype(F32).astype(BF16).reshape(8, 16, 128)
            for b in range(count):
                here = jnp.where(high == (base + b).astype(F32).astype(BF16), one, zero)[None]
                pick_ref[b * 128 : (b + 1) * 128, line * 128 : (line + 1) * 128] = (low * here).reshape(128, 128)

    build(0)
    total = jnp.zeros(sum_ref.shape, F32)
    for q in range(pieces):
        if q + 1 < pieces:
            build(q + 1)
        at = slice(q * lines * 128, (q + 1) * lines * 128)
        total = total + dot(pick_ref[:, at], incoming_ref[at, :])
    sum_ref[...] = total * scale_ref[0]


def scatter(scale, named, incoming, vocab):
    step = 1024
    width = incoming.shape[1]
    return pl.pallas_call(
        scatter_kernel,
        grid=(vocab // step,),
        out_shape=jax.ShapeDtypeStruct((vocab, width), F32),
        in_specs=[
            pl.BlockSpec(memory_space=pltpu.SMEM),
            pl.BlockSpec(named.shape, lambda i: (0, 0)),
            pl.BlockSpec(incoming.shape, lambda i: (0, 0)),
        ],
        out_specs=pl.BlockSpec((step, width), lambda i: (i, 0)),
        scratch_shapes=[pltpu.VMEM((step, named.shape[0] * 128), BF16)],
        compiler_params=params(48),
    )(scale, named, incoming)


def smooth(v):
    c = jnp.clip(v, -SMOOTH_HALF, SMOOTH_HALF)
    return -0.002 * c * c * c + 0.15 * c + 0.5


def smooth_slope(v):
    c = jnp.clip(v, -SMOOTH_HALF, SMOOTH_HALF)
    inside = jnp.where((v >= -SMOOTH_HALF) & (v <= SMOOTH_HALF), 1.0, 0.0)
    return inside * (0.15 - 0.006 * c * c)


def main_kernel(
    scale_ref,
    core_ref,
    active_ref,
    b_in_ref,
    b_out_ref,
    gates_ref,
    target_ref,
    replied_ref,
    cot_hbm,
    w_in_hbm,
    w_out_hbm,
    keep_in_hbm,
    keep_out_hbm,
    send_in_hbm,
    send_out_hbm,
    outgoing_hbm,
    mixed_hbm,
    small_ref,
    small_low,
    outgoing_ref,
    mixed_ref,
    fill_ref,
    pick_ref,
    cot_ref,
    w_in_ref,
    w_out_ref,
    result_ref,
    hidden_ref,
    hidden_up_ref,
    w_in_low,
    w_out_low,
    b_in_sum,
    b_out_sum,
    in_sem,
    out_sem,
):
    rows = active_ref.shape[1]
    part = 64
    blocks = rows // part
    flat = part * NTASK
    slots, width = replied_ref.shape
    hidden_width = w_in_ref.shape[2]
    chunk = 256
    chunks = hidden_width // chunk
    half = EXPERTS // 2
    zero16 = jnp.bfloat16(0)

    loads = {}

    def load(name, source, target):
        loads[name] = pltpu.make_async_copy(source, target, in_sem.at[len(loads)])
        loads[name].start()

    def loaded(name):
        if name in loads:
            loads.pop(name).wait()

    load(("in", 0), w_in_hbm.at[0], w_in_ref.at[0])
    load("cot", cot_hbm, cot_ref)
    load(("out", 0), w_out_hbm.at[0], w_out_ref.at[0])
    for e in range(1, EXPERTS):
        load(("in", e), w_in_hbm.at[e], w_in_ref.at[e])
        load(("out", e), w_out_hbm.at[e], w_out_ref.at[e])

    stores = []

    def store(source, target):
        stores.append(pltpu.make_async_copy(source, target, out_sem.at[len(stores)]))
        stores[-1].start()

    target = target_ref[...]
    columns = jnp.transpose(jnp.concatenate([target >> 7, target & 127] * 2, axis=0).astype(F32), (1, 0))

    def spread(k):
        return jnp.broadcast_to(columns[:, k : k + 1], (rows, 128))

    highs = [spread(f).astype(BF16) for f in range(2)]
    lows = [(spread(2 + f).astype(I32) == iota((rows, 128), 1)).astype(F32).astype(BF16) for f in range(2)]
    pieces = 4
    lines = slots // 128 // pieces

    def pick(p):
        for b in range(p * lines, (p + 1) * lines):
            first = jnp.where(highs[0] == jnp.bfloat16(b), lows[0], zero16)
            pick_ref[:, b * 128 : (b + 1) * 128] = jnp.where(highs[1] == jnp.bfloat16(b), lows[1], first)

    inputs = jnp.zeros((rows, width), F32)
    wide_rows = rows // 128
    at_high, at_low = [], []
    for piece in range(wide_rows):
        at = target[:, piece * 128 : (piece + 1) * 128]
        at_high.append([jnp.broadcast_to(at[f : f + 1, :] >> 7, (16, 128)).astype(F32).astype(BF16) for f in range(2)])
        low = [(at[f : f + 1, :] & 127) == iota((128, 128), 0) for f in range(2)]
        at_low.append([x.astype(F32).astype(BF16).reshape(8, 16, 128) for x in low])

    def fill(line):
        for piece in range(wide_rows):
            here = [jnp.where(h == jnp.bfloat16(line), jnp.bfloat16(1), zero16)[None] for h in at_high[piece]]
            fill_ref[line * 128 : (line + 1) * 128, piece * 128 : (piece + 1) * 128] = (
                at_low[piece][0] * here[0] + at_low[piece][1] * here[1]
            ).reshape(128, 128)

    for line in range(slots // 128):
        fill(line)
    inputs_t = dot(replied_ref[...], fill_ref[...], TN).astype(BF16)
    inputs = jnp.transpose(inputs_t, (1, 0))

    gates_w = gates_ref[...]
    once = jnp.where((iota(gates_w.shape, 0) & 4) == 0, gates_w, zero16)
    logits = dot(gates_w, inputs, NT)
    active = active_ref[...]
    active = jnp.concatenate([active, active], axis=0)
    along = iota((part, flat), 0) == (iota((part, flat), 1) >> 2)
    repeat = along.astype(F32).astype(BF16)
    own_task = iota((8, flat), 0) == (iota((8, flat), 1) & 3)

    def group(k):
        return logits[8 * k : 8 * k + 8, :]

    zetas = [[group(n * KSEL + c) for c in range(KSEL)] for n in range(BITS)]
    levels = [[smooth(z) for z in zs] for zs in zetas]
    mix = [group(BITS * KSEL + c) for c in range(KSEL)]
    top = jnp.maximum(jnp.maximum(mix[0], mix[1]), jnp.maximum(mix[2], mix[3]))
    mix = [jnp.exp(m - top) for m in mix]
    total = 1.0 / (mix[0] + mix[1] + mix[2] + mix[3])
    mix = [m * total for m in mix]
    chosen = [
        [
            (levels[0][c] if e & 1 else 1.0 - levels[0][c]) * (levels[1][c] if e & 2 else 1.0 - levels[1][c])
            for e in range(EXPERTS)
        ]
        for c in range(KSEL)
    ]
    gate = [sum(mix[c] * chosen[c][e] for c in range(KSEL)) * active for e in range(EXPERTS)]

    loaded("cot")
    ups, gate_rows = [], []
    for b in range(blocks):
        g = [x[:, b * part : (b + 1) * part] for x in gate]
        gate_rows.append(jnp.concatenate(g, axis=1).astype(BF16))
        wide = dot(jnp.concatenate(g, axis=0).astype(BF16), repeat)
        mats = []
        for e in range(EXPERTS):
            row = jnp.sum(jnp.where(own_task, wide[8 * e : 8 * e + 8, :], 0.0), axis=0, keepdims=True)
            row = jnp.broadcast_to(row, (part, flat)).astype(BF16)
            mats.append(jnp.where(along, row, zero16))
        cot = cot_ref[b * part : (b + 1) * part].reshape(flat, width)
        ups.append(dot(jnp.concatenate(mats, axis=0), cot))
    result_up = [jnp.concatenate([u[e * part : (e + 1) * part, :] for u in ups], axis=0) for e in range(EXPERTS)]
    result_low = [u.astype(BF16) for u in result_up]

    def into_tiles(low, e, part):
        part = part * scale_ref[0]
        per = width // 16
        for q in range(hidden_width // 128):
            low[e, q * per : (q + 1) * per] = part[:, q * 128 : (q + 1) * 128].astype(BF16).reshape(per, 16, 128)

    def first_layer(e, c):
        loaded(("in", e))
        loaded(("out", e))
        at = slice(c * chunk, (c + 1) * chunk)
        pre = dot(inputs, w_in_ref[e, :, at]) + b_in_ref[e : e + 1, at].astype(F32)
        logistic = 0.5 * jnp.tanh(0.5 * pre) + 0.5
        hidden = pre * logistic
        slope = logistic + hidden - hidden * logistic
        hidden_ref[e % 2, :, at] = hidden.astype(BF16)
        hidden_up = dot(result_low[e], w_out_ref[e, at, :], NT) * slope
        b_in_sum[e : e + 1, at] = jnp.sum(hidden_up, axis=0, keepdims=True)
        hidden_up_ref[e % 2, :, at] = hidden_up.astype(BF16)

    input_up = jnp.zeros((rows, width), F32)

    def second_layer(e, c):
        nonlocal input_up
        if c == 0:
            result = dot(hidden_ref[e % 2], w_out_ref[e]) + b_out_ref[e : e + 1, :].astype(F32)
            result = result.astype(BF16)
            result_ref[:, e] = result.reshape(blocks, part, width)
            b_out_sum[e : e + 1, :] = jnp.sum(result_up[e], axis=0, keepdims=True)
        elif c == 1:
            input_up = input_up + dot(hidden_up_ref[e % 2], w_in_ref[e], NT)
        elif c == 2:
            into_tiles(w_in_low, e, dot(inputs_t, hidden_up_ref[e % 2]))
        else:
            into_tiles(w_out_low, e, dot(jnp.transpose(result_low[e], (1, 0)), hidden_ref[e % 2]))

    for c in range(chunks):
        first_layer(0, c)
    for e in range(EXPERTS):
        for c in range(chunks):
            if e + 1 < EXPERTS:
                first_layer(e + 1, c)
            second_layer(e, c)

    core = core_ref[0]
    tiles = w_in_low.shape[1]
    for i in range(half):
        mine = core * half + i
        other = (1 - core) * half + i
        at = pl.ds(i * tiles, tiles)
        store(w_in_low.at[mine], keep_in_hbm.at[at])
        store(w_out_low.at[mine], keep_out_hbm.at[at])
        store(w_in_low.at[other], send_in_hbm.at[at])
        store(w_out_low.at[other], send_out_hbm.at[at])

    down = (iota((flat, flat), 0) >> 2) == (iota((flat, flat), 1) & (part - 1))
    gate_up = [[] for _ in range(EXPERTS)]
    for b in range(blocks):
        cot = cot_ref[b * part : (b + 1) * part].reshape(flat, width)
        products = jnp.where(down, dot(cot, result_ref[b].reshape(flat, width), NT), 0.0)
        p = jnp.sum(products.reshape(flat // 8, 8, flat), axis=0)
        p = p + jnp.concatenate([p[4:], p[:4]], axis=0)
        for e in range(EXPERTS):
            gate_up[e].append(p[:, e * part : (e + 1) * part])
    gate_up = [jnp.concatenate(g, axis=1) * active for g in gate_up]
    level_up = [[None] * KSEL for _ in range(BITS)]
    mixing_up = []
    entropy = 0.0
    for c in range(KSEL):
        mixing_up.append(sum(gate_up[e] * chosen[c][e] for e in range(EXPERTS)))
        chosen_up = []
        for e in range(EXPERTS):
            x = chosen[c][e]
            log = jnp.log(x + LOG_GUARD)
            entropy = entropy - x * log
            chosen_up.append(gate_up[e] * mix[c] - (ENTROPY_WEIGHT * active) * (log + x / (x + LOG_GUARD)))
        l0, l1 = levels[0][c], levels[1][c]
        level_up[0][c] = (chosen_up[1] - chosen_up[0]) * (1.0 - l1) + (chosen_up[3] - chosen_up[2]) * l1
        level_up[1][c] = (chosen_up[2] - chosen_up[0]) * (1.0 - l0) + (chosen_up[3] - chosen_up[1]) * l0
    entropy = (active * entropy)[:4, :]
    mean_up = sum(mixing_up[c] * mix[c] for c in range(KSEL))
    ups_all = [level_up[n][c] * smooth_slope(zetas[n][c]) for n in range(BITS) for c in range(KSEL)]
    ups_all += [mix[c] * (mixing_up[c] - mean_up) for c in range(KSEL)]
    logits_up = jnp.concatenate(ups_all, axis=0)
    up_high = logits_up.astype(BF16)
    up_low = (logits_up - up_high.astype(F32)).astype(BF16)
    input_up = (input_up + dot(up_high, once, TN) + dot(up_low, once, TN)).astype(BF16)
    for b in range(blocks):
        mats = jnp.where(down, jnp.concatenate([gate_rows[b]] * (flat // 8), axis=0), zero16)
        mixed = dot(mats, result_ref[b].reshape(flat, width))
        mixed_ref[b * part : (b + 1) * part] = mixed.reshape(part, NTASK, width).astype(BF16)
    store(mixed_ref, mixed_hbm)
    span = slots // pieces
    for p in range(pieces):
        at = pl.ds(p * span, span)
        outgoing_ref[at, :] = dot(fill_ref[at, :], input_up).astype(BF16)
        store(outgoing_ref.at[at], outgoing_hbm.at[at])

    scale = scale_ref[0]
    gates_sum = (dot(up_high, inputs) + dot(up_low, inputs)) * scale
    small_ref[...] = jnp.zeros_like(small_ref)
    n = 0

    def put(values):
        nonlocal n
        for q in range(values.shape[1] // 128):
            small_ref[n // 4, n % 4 * 4 : n % 4 * 4 + 4, :] = values[:, q * 128 : (q + 1) * 128]
            n += 1

    for k in range(12):
        put(gates_sum[8 * k : 8 * k + 4, :])
    put(b_out_sum[...] * scale)
    put(b_in_sum[...] * scale)
    put(entropy)
    small_low[...] = small_ref[...].astype(BF16)
    share = small_low.shape[0] // 2
    at = pl.ds(half * tiles, share)
    store(small_low.at[pl.ds(core * share, share)], keep_in_hbm.at[at])
    store(small_low.at[pl.ds((1 - core) * share, share)], send_in_hbm.at[at])
    for copy in stores:
        copy.wait()


def experts(scale, core, active, target, replied, cot, w_in, b_in, w_out, b_out, gates, share):
    rows, slots = active.shape[1], replied.shape[0]
    width, hidden = w_in.shape[1], w_in.shape[2]
    smem = pl.BlockSpec(memory_space=pltpu.SMEM)
    hbm = pl.BlockSpec(memory_space=pl.ANY)
    tiles = width * hidden // 2048
    grads = jax.ShapeDtypeStruct((EXPERTS // 2 * tiles, 16, 128), BF16)
    grads_small = jax.ShapeDtypeStruct((EXPERTS // 2 * tiles + share, 16, 128), BF16)
    low = pltpu.VMEM((EXPERTS, tiles, 16, 128), BF16)
    act = pltpu.VMEM((2, rows, hidden), BF16)
    result = (rows // 64, EXPERTS, 64, width)
    near = pltpu.with_memory_space_constraint(replied, pltpu.VMEM)
    return pl.pallas_call(
        main_kernel,
        out_shape=(
            grads_small,
            grads,
            grads_small,
            grads,
            jax.ShapeDtypeStruct((slots, width), BF16),
            jax.ShapeDtypeStruct(cot.shape, BF16),
        ),
        in_specs=[smem, smem] + [VMEM] * 6 + [hbm] * 3,
        out_specs=(hbm,) * 6,
        scratch_shapes=[
            pltpu.VMEM((2 * share, 16, 128), F32),
            pltpu.VMEM((2 * share, 16, 128), BF16),
            pltpu.VMEM((slots, width), BF16),
            pltpu.VMEM(cot.shape, BF16),
            pltpu.VMEM((slots, rows), BF16),
            pltpu.VMEM((rows, slots), BF16),
            pltpu.VMEM(cot.shape, BF16),
            pltpu.VMEM(w_in.shape, BF16),
            pltpu.VMEM(w_out.shape, BF16),
            pltpu.VMEM(result, BF16),
            act,
            act,
            low,
            low,
            pltpu.VMEM((EXPERTS, hidden), F32),
            pltpu.VMEM((EXPERTS, width), F32),
            pltpu.SemaphoreType.DMA((1 + 2 * EXPERTS,)),
            pltpu.SemaphoreType.DMA((4 * EXPERTS // 2 + 7,)),
        ],
        compiler_params=params(56),
    )(scale, core, active, b_in, b_out, gates, target, near, cot, w_in, w_out)


def swap(x, mask, devices):
    return lax.ppermute(x, AXES, [(i, i ^ mask) for i in range(devices)])


def bits_of(count):
    return range(count.bit_length() - 1)


def sum_over_devices(x, devices):
    for k in bits_of(devices):
        x = x + swap(x, 1 << k, devices)
    return x


def halves(x, bit):
    rows = x.shape[0] // 2
    keep = lax.dynamic_slice_in_dim(x, bit * rows, rows, 0)
    give = lax.dynamic_slice_in_dim(x, (1 - bit) * rows, rows, 0)
    return keep, give.astype(BF16)


def joined(mine, other, bit):
    return jnp.where(bit == 0, jnp.concatenate([mine, other]), jnp.concatenate([other, mine]))


def tied(*values):
    return lax.optimization_barrier(values)


def sum_weights(keeps, sends, tiles, incoming, index, dp_count, outer_count):
    devices = dp_count * outer_count
    core = outer_count
    outer = [1 << k for k in bits_of(outer_count)]
    across = [outer_count << k for k in bits_of(dp_count)][1:]
    first = [outer[0], across[0]]
    rest = outer[1:] + across[1:]

    def bit(mask):
        return (index // mask) % 2

    pieces = []
    for keep, send in zip(keeps, sends):
        whole = keep.astype(F32) + swap(send, core, devices).astype(F32)
        pieces.append([whole[:tiles], whole[tiles:]])
    for orders in (first, first[::-1]):
        for n, parts in enumerate(pieces):
            split = [halves(p, bit(m)) for p, m in zip(parts, orders)]
            pieces[n] = [k + swap(g, m, devices).astype(F32) for (k, g), m in zip(split, orders)]
    for mask in rest:
        for n, parts in enumerate(pieces):
            split = [halves(p, bit(mask)) for p in parts]
            cut = split[0][0].shape[0]
            got = swap(jnp.concatenate([g for _, g in split]), mask, devices).astype(F32)
            pieces[n] = [split[0][0] + got[:cut], split[1][0] + got[cut:]]
    pieces = [[p.astype(BF16) for p in parts] for parts in pieces]
    for mask in rest[::-1]:
        for n, parts in enumerate(pieces):
            cut = parts[0].shape[0]
            got = swap(jnp.concatenate(parts), mask, devices)
            pieces[n] = [joined(parts[0], got[:cut], bit(mask)), joined(parts[1], got[cut:], bit(mask))]
    for step, orders in enumerate((first[::-1], first)):
        pieces = [[joined(p, swap(p, m, devices), bit(m)) for p, m in zip(parts, orders)] for parts in pieces]
        if step == 0:
            pieces, incoming = tied(pieces, incoming)
    return [jnp.concatenate(parts) for parts in pieces], incoming


def spread(sums_in_ref, sums_out_ref, w_in_ref, w_out_ref):
    width, hidden = w_in_ref.shape[1:]
    per = width // 16
    for q in range(hidden // 128):
        at = slice(q * 128, (q + 1) * 128)
        w_in_ref[0, :, at] = sums_in_ref[q * per : (q + 1) * per].astype(F32).reshape(width, 128)
        out = sums_out_ref[q * per : (q + 1) * per].astype(F32).reshape(width, 128)
        w_out_ref[0, at, :] = jnp.transpose(out, (1, 0))


def place_kernel(core_ref, sums_in_ref, sums_out_ref, w_in_ref, w_out_ref):
    spread(sums_in_ref, sums_out_ref, w_in_ref, w_out_ref)


def last_kernel(
    core_ref,
    sums_in_ref,
    sums_out_ref,
    mine_ref,
    other_ref,
    scale_ref,
    _,
    __,
    w_in_ref,
    w_out_ref,
    select_ref,
    mix_ref,
    b_in_ref,
    b_out_ref,
    entropy_ref,
    small_ref,
):
    spread(sums_in_ref, sums_out_ref, w_in_ref, w_out_ref)

    @pl.when(pl.program_id(0) == 0)
    def _():
        share = mine_ref.shape[0]
        small_ref[pl.ds((1 - core_ref[0]) * share, share)] = mine_ref[...].astype(F32)
        small_ref[pl.ds(core_ref[0] * share, share)] = other_ref[...].astype(F32)
        n = 0

        def take(blocks):
            nonlocal n
            got = [small_ref[(n + q) // 4, (n + q) % 4 * 4 : (n + q) % 4 * 4 + 4, :] for q in range(blocks)]
            n += blocks
            return got

        width = b_out_ref.shape[1]
        lanes = width // 128
        for k in range(BITS * KSEL + KSEL):
            got = jnp.concatenate(take(lanes), axis=1)
            for t in range(NTASK):
                if k < BITS * KSEL:
                    row = t * KSEL * BITS + k % KSEL * BITS + k // KSEL
                    select_ref[row : row + 1, :] = got[t : t + 1, :]
                else:
                    row = t * KSEL + k % KSEL
                    mix_ref[row : row + 1, :] = got[t : t + 1, :]
        b_out_ref[...] = jnp.concatenate(take(lanes), axis=1)
        b_in_ref[...] = jnp.concatenate(take(b_in_ref.shape[1] // 128), axis=1)
        total = jnp.sum(sum(take(4 * SMALL - n)), axis=0, keepdims=True)
        entropy_ref[...] = jnp.sum(total, axis=1, keepdims=True) * scale_ref[0]


def place(core, width, hidden, sums_in, sums_out, before=(), small=()):
    half = EXPERTS // 2
    tiles = width * hidden // 2048
    shapes = ((EXPERTS, width, hidden), (EXPERTS, hidden, width))
    one = pl.BlockSpec((tiles, 16, 128), lambda i, c: (i, 0, 0))
    out_specs = tuple(pl.BlockSpec((1,) + s[1:], lambda i, c: (c[0] * half + i, 0, 0)) for s in shapes)
    in_specs = [one, one]
    scratch = []
    if small:
        rest = ((NTASK * KSEL * BITS, width), (NTASK * KSEL, width), (EXPERTS, hidden), (EXPERTS, width), (1, 1))
        shapes += rest
        out_specs += tuple(pl.BlockSpec(s, lambda i, c: (0, 0)) for s in rest)
        share = small[0].shape[0] - half * tiles
        in_specs += [pl.BlockSpec((share, 16, 128), lambda i, c: (half * tiles // share, 0, 0))] * 2
        in_specs.append(pl.BlockSpec(memory_space=pltpu.SMEM))
        scratch = [pltpu.VMEM((2 * share, 16, 128), F32)]
    return pl.pallas_call(
        last_kernel if small else place_kernel,
        grid_spec=pltpu.PrefetchScalarGridSpec(
            num_scalar_prefetch=1,
            grid=(half,),
            in_specs=in_specs + [HBM] * len(before),
            out_specs=out_specs,
            scratch_shapes=scratch,
        ),
        out_shape=tuple(jax.ShapeDtypeStruct(s, F32) for s in shapes),
        input_output_aliases={1 + len(in_specs) + k: k for k in range(len(before))},
        compiler_params=params(32),
    )(core, sums_in, sums_out, *small, *before)


def on_device(
    table,
    source_id,
    task_mask,
    feature_owner,
    feature_row,
    w_in,
    b_in,
    w_out,
    b_out,
    select_weight,
    mix_weight,
    cotangent,
):
    rows = source_id.shape[0]
    dp_count, outer_count = lax.axis_size("dp"), lax.axis_size("outer")
    devices = dp_count * outer_count
    index = lax.axis_index("dp") * outer_count + lax.axis_index("outer")
    vocab, width = table.shape
    per_row = feature_owner.shape[1]
    cap = 2 * per_row * rows // devices
    slots = devices * cap

    def exchange(x):
        return lax.all_to_all(x, AXES, split_axis=0, concat_axis=0, tiled=True)

    request, target, active = prepare(
        source_id.reshape(1, rows), task_mask.T, feature_owner.T, feature_row.T, devices, cap
    )
    arrived = exchange(request).reshape(devices, 2 * cap)
    weight_rows = (jnp.float32(rows * devices) / jnp.sum(arrived[:, cap]).astype(F32)).reshape(1)
    named = arrived if cap == 128 else arrived[:, :cap].reshape(slots // 128, 128)
    found = find(named, table)
    replied = exchange(found.reshape(devices, cap, width)).reshape(slots, width)

    select = select_weight.T.reshape(NTASK, KSEL, BITS, width).transpose(2, 1, 0, 3)
    mix = mix_weight.T.reshape(NTASK, KSEL, width).transpose(1, 0, 2)
    gates = jnp.concatenate([select.reshape(BITS * KSEL, NTASK, width), mix])
    gates = jnp.concatenate([gates, gates], axis=1).reshape(-1, width)
    core = (index // outer_count) % 2
    share = -(-SMALL // devices) * devices // 2
    keep_in, keep_out, send_in, send_out, outgoing, mixed = experts(
        weight_rows,
        core.reshape(1).astype(I32),
        active,
        target,
        replied,
        cotangent,
        w_in,
        b_in,
        w_out,
        b_out,
        gates,
        share,
    )

    incoming = exchange(outgoing.reshape(devices, cap, width)).reshape(slots, width)
    (mine_in, mine_out), incoming = sum_weights(
        (keep_in, keep_out), (send_in, send_out), width * w_in.shape[2] // 2048, incoming, index, dp_count, outer_count
    )
    table_sum = scatter(weight_rows, named, incoming, vocab)
    mine_in, mine_out, table_sum = tied(mine_in, mine_out, table_sum)
    core_here = core.reshape(1).astype(I32)
    hidden = w_in.shape[2]
    placed = place(core_here, width, hidden, mine_in, mine_out)
    others = [swap(m, outer_count, devices) for m in (mine_in, mine_out)]
    w_in_sum, w_out_sum, select_sum, mix_sum, b_in_sum, b_out_sum, entropy = place(
        1 - core_here, width, hidden, *others, placed, (mine_in, others[0], weight_rows / (rows * devices))
    )
    return (
        mixed,
        table_sum,
        w_in_sum,
        b_in_sum,
        w_out_sum,
        b_out_sum,
        select_sum.T,
        mix_sum.T,
        entropy.reshape(()),
    )


def solution(mesh):
    rows = P(AXES)
    flat = P(AXES, None)
    cube = P(AXES, None, None)
    placed = (flat, rows, P(), flat, flat, P(), P(), P(), P(), P(), P(), cube)
    return jax.shard_map(
        on_device,
        mesh=mesh,
        in_specs=placed,
        out_specs=(cube, flat, P(), P(), P(), P(), P(), P(), P()),
        check_vma=False,
    )
```
